32 devices in a mesh: tile: 4 (over y, x), cand: 1, group: 8 (over z, core).
Axes of the slice: x: 2, y: 2, z: 4, core: 2. Of those that a mesh axis runs over, the one named last changes fastest.
Arguments:
- latent: bfloat16 [32, 12, 48, 384], P(('cand', 'group'), 'tile'), may hold values from -6 to 6
- gain_first: float32 [384], replicated, may hold values from 0.25 to 1.75
- weight_first: bfloat16 [3, 3, 1152, 384], P(None, None, 'group'), may hold values from -0.0625 to 0.0625
- bias_first: float32 [384], replicated, may hold values from -0.6 to 0.6
- gain_second: float32 [384], replicated, may hold values from 0.25 to 1.75
- weight_second: bfloat16 [3, 3, 1152, 384], P(None, None, 'group'), may hold values from -0.0625 to 0.0625
- bias_second: float32 [384], replicated, may hold values from -0.6 to 0.6
Outputs:
- decoded: bfloat16 [32, 12, 48, 384], P(('cand', 'group'), 'tile')
The draws below stay inside these ranges and needn't reach their ends.
All inputs are finite; a program needn't handle non-finite values.
Results may differ from the reference program's by a relative error of at most 0.0042.
Values may be sent and summed in bfloat16 or wider, within the bound.
A program may use at most 128 MiB of HBM per device.

```python
import jax
import jax.numpy as jnp
from jax import lax

C = 384
WID = 48
FRAMES = 32
ROWS = 12


def level_of(own_key, dims, shards, low, top_value):
    loudness, own = 1.0, jax.random.fold_in(own_key, 6)
    for axis_at, parts in shards:
        heights = jnp.exp(jax.random.uniform(jax.random.fold_in(own, axis_at), (parts,), jnp.float32, low / len(shards), top_value / len(shards)))
        loudness = loudness * jnp.repeat(heights, dims[axis_at] // parts).reshape([-1 if axis == axis_at else 1 for axis in range(len(dims))])
    return loudness


def scatter_about(key, extent, scale, most, split=(), dtype=jnp.bfloat16):
    level = level_of(key, extent, split, -0.22, 0.18) if split else 1.0
    array = jax.random.normal(key, extent, jnp.float32) * scale * level
    return jnp.minimum(jnp.maximum(array, -most), most).astype(dtype)


def setup_inputs(seed: int = 0, part: int = 0) -> dict:
    streams_of = jax.random.split(jax.random.key(seed), 8)
    part_keys = jax.random.split(jax.random.fold_in(streams_of[7], part), 8)
    return {
        "latent": scatter_about(part_keys[0], (FRAMES, ROWS, WID, C), 1.0, 6.0, ((0, 8), (1, 4))),
        "gain_first": jnp.clip(1.0 + 0.15 * jax.random.normal(streams_of[1], (C,), jnp.float32), 0.25, 1.75),
        "weight_first": scatter_about(streams_of[2], (3, 3, 3 * C, C), (27 * C) ** -0.5, 0.0625, ((2, 8),)),
        "bias_first": jnp.clip(jax.random.uniform(streams_of[3], (C,), jnp.float32, -0.6, 0.6), -0.6, 0.6),
        "gain_second": jnp.clip(1.0 + 0.15 * jax.random.normal(streams_of[4], (C,), jnp.float32), 0.25, 1.75),
        "weight_second": scatter_about(streams_of[5], (3, 3, 3 * C, C), (27 * C) ** -0.5, 0.0625, ((2, 8),)),
        "bias_second": jnp.clip(jax.random.uniform(streams_of[6], (C,), jnp.float32, -0.6, 0.6), -0.6, 0.6),
    }


def activate(values, gain):
    wide = values.astype(jnp.float32)
    scaled = wide * jax.lax.rsqrt(lax.optimization_barrier(jnp.mean(wide * wide, axis=-1, keepdims=True)) + 1e-06) * gain
    return jax.nn.silu(scaled)

def taps(padded, weight):
    count = padded.shape[0] - 2
    tall = padded.shape[1] - 2
    across = padded.shape[2] - 2
    chans = padded.shape[3]
    total = jnp.zeros((count * tall * across, weight.shape[3]), jnp.float32)
    for step_t in range(3):
        for step_r in range(3):
            window = padded[step_t:step_t + count, step_r:step_r + tall]
            joined = jnp.concatenate([window[:, :, k:k + across] for k in range(3)], axis=-1)
            joined = joined.reshape(-1, 3 * chans).astype(jnp.float32)
            total = total + jnp.dot(joined, weight[step_t, step_r].astype(jnp.float32), preferred_element_type=jnp.float32)
    return total.reshape(count, tall, across, weight.shape[3])

def reference(latent, gain_first, weight_first, bias_first, gain_second, weight_second, bias_second):
    first = activate(latent, gain_first).astype(jnp.bfloat16)
    padded = jnp.pad(first, ((2, 0), (1, 1), (1, 1), (0, 0)))
    hidden = taps(padded, weight_first) + bias_first
    second = activate(hidden, gain_second).astype(jnp.bfloat16)
    padded = jnp.pad(second, ((2, 0), (1, 1), (1, 1), (0, 0)))
    result = latent.astype(jnp.float32) + taps(padded, weight_second) + bias_second
    return result.astype(jnp.bfloat16)
```

```python
import jax
import jax.numpy as jnp
from jax import lax
from jax.experimental import pallas as pl
from jax.experimental.pallas import tpu as pltpu
from jax.sharding import PartitionSpec as P


def shifted(value, axis, steps):
    count = lax.axis_size(axis)
    first, last = (max(0, -steps), min(count, count - steps))
    return lax.ppermute(value, axis, [(source, source + steps) for source in range(first, last)])


def with_halo(array, sides, width):
    for axis, dim in sides:
        size, length = (lax.axis_size(axis), array.shape[dim])
        up = [(i, (i + 1) % size) for i in range(size - 1)]
        down = [(j, i) for i, j in up]
        last = lax.slice_in_dim(array, length - width, length, axis=dim)
        first = lax.slice_in_dim(array, 0, width, axis=dim)
        before = lax.ppermute(last, axis, up)
        after = lax.ppermute(first, axis, down)
        array = jnp.concatenate([before, array, after], axis=dim)
    return array


def activate(values, gain):
    wide = values.astype(jnp.float32)
    scaled = wide * lax.rsqrt(jnp.mean(wide * wide, axis=-1, keepdims=True) + 1e-06) * gain
    return jax.nn.silu(scaled)


def widen(grown):
    across = grown.shape[2]
    padded = jnp.pad(grown, ((0, 0), (0, 0), (1, 1), (0, 0)))
    return jnp.concatenate([padded[:, :, k : k + across] for k in range(3)], axis=-1)


def taps(joined, piece):
    count = joined.shape[0] - 2
    tall = joined.shape[1] - 2
    across = joined.shape[2]
    inner = piece.shape[2]
    total = jnp.zeros((count * tall * across, piece.shape[3]), jnp.float32)
    for step_t in range(3):
        for step_r in range(3):
            window = joined[step_t : step_t + count, step_r : step_r + tall].reshape(-1, inner)
            total = total + jnp.dot(
                window, piece[step_t, step_r], preferred_element_type=jnp.float32
            )
    return total.reshape(count, tall, across, piece.shape[3])


def local(latent, gain_first, weight_first, bias_first, gain_second, weight_second, bias_second):
    frames, rows, width, chans = latent.shape
    depth = 1
    first = activate(latent, gain_first).astype(jnp.bfloat16)
    earlier = shifted(first[frames - 2 :], "group", 1)
    stacked = jnp.concatenate([earlier, first], axis=0)
    grown = with_halo(stacked, (("tile", 1),), depth)
    joined_first = widen(grown)
    hidden = (
        taps(joined_first, lax.all_gather(weight_first, "group", axis=2, tiled=True)) + bias_first
    )
    second = activate(hidden, gain_second)
    second = second.astype(jnp.bfloat16)
    later = shifted(second[frames - 2 :], "group", 1)
    second = jnp.concatenate([later, second], axis=0)
    second = with_halo(second, (("tile", 1),), 1)
    joined_second = widen(second)
    branch = taps(joined_second, lax.all_gather(weight_second, "group", axis=2, tiled=True))
    result = latent.astype(jnp.float32) + branch + bias_second
    return result.astype(jnp.bfloat16)


BF16, F32 = jnp.bfloat16, jnp.float32
MESH = pl.DeviceIdType.MESH
UNITS = 6


def act_slab(wide, gain):
    square = jnp.sum(wide * wide, axis=-1, keepdims=True) * (1.0 / wide.shape[-1])
    scaled = wide * lax.rsqrt(square + 1e-06) * gain
    return scaled / (1.0 + jnp.exp(-scaled))


def fused(
    latent, gain_first, weight_first, bias_first, gain_second, weight_second, bias_second, out,
    taps_all, lat, sec, cols, total,
    load_sem, lat_sem, z_send, z_recv, xy_send, xy_recv, core_send, core_recv, halo_send, halo_recv,
):
    tile, group = lax.axis_index("tile"), lax.axis_index("group")
    tiles, groups = lax.axis_size("tile"), lax.axis_size("group")
    y, x = tile // 2, tile % 2
    z, core = group // 2, group % 2
    zs = groups // 2
    frames, rows, across, chans = latent.shape
    x_tile, y_tile = 2 * y + (1 - x), 2 * (1 - y) + x
    z_part = x + 2 * y - 3 * x * y
    x_part = x + 2 * y - 2 * x * y
    y_part = x + 2 * y - x * y
    corner = (x + y) == 2

    lat[...] = jnp.zeros_like(lat)
    sec[...] = jnp.zeros_like(sec)
    total[...] = jnp.zeros_like(total)

    def load(unit):
        source = weight_first if unit < 3 else weight_second
        return pltpu.make_async_copy(
            source.at[pl.ds(3 * (unit % 3), 3)],
            taps_all.at[pl.ds(3 * unit, 3), z, core],
            load_sem.at[unit],
        )

    lat_copy = pltpu.make_async_copy(
        latent, lat.at[pl.ds(2, frames), pl.ds(1, rows)], lat_sem
    )
    for unit in range(UNITS):
        load(unit).start()
    lat_copy.start()

    barrier = pltpu.get_barrier_semaphore()
    partners = [
        ({"group": group + 2}, z < zs - 1),
        ({"group": group - 2}, z > 0),
        ({"group": group + 1}, group < groups - 1),
        ({"group": group - 1}, group > 0),
        ({"tile": tile + 1}, tile < tiles - 1),
        ({"tile": tile - 1}, tile > 0),
        ({"tile": x_tile}, None),
        ({"tile": y_tile}, None),
    ]
    expected = 0
    for where, there in partners:
        if there is None:
            pl.semaphore_signal(barrier, inc=1, device_id=where, device_id_type=MESH)
            expected = expected + 1
        else:
            @pl.when(there)
            def _():
                pl.semaphore_signal(barrier, inc=1, device_id=where, device_id_type=MESH)
            expected = expected + there.astype(jnp.int32)
    pl.semaphore_wait(barrier, expected)

    def piece(unit, part, origin, where, send, recv):
        block = taps_all.at[3 * unit + part, origin, core]
        return pltpu.make_async_remote_copy(
            src_ref=block, dst_ref=block, send_sem=send, recv_sem=recv,
            device_id=where, device_id_type=MESH,
        )

    def up(unit, dist):
        return piece(unit, z_part, z - dist, {"group": group + 2}, z_send.at[unit, 0, dist], z_recv.at[unit, 0, dist])

    def down(unit, dist):
        return piece(unit, z_part, z + dist, {"group": group - 2}, z_send.at[unit, 1, dist], z_recv.at[unit, 1, dist])

    def along_x(unit, step):
        return piece(unit, x_part, (z + step) % zs, {"tile": x_tile}, xy_send.at[unit, 0, step - 1], xy_recv.at[unit, 0, step - 1])

    def along_y(unit, step):
        return piece(unit, y_part, (z + step) % zs, {"tile": y_tile}, xy_send.at[unit, 1, step - 1], xy_recv.at[unit, 1, step - 1])

    def across_cores(unit):
        block = taps_all.at[pl.ds(3 * unit, 3), :, core]
        return pltpu.make_async_remote_copy(
            src_ref=block, dst_ref=block, send_sem=core_send.at[unit], recv_sem=core_recv.at[unit],
            device_id={"group": 2 * z + (1 - core)}, device_id_type=MESH,
        )

    def own(unit):
        @pl.when(z < zs - 1)
        def _():
            up(unit, 0).start()

        @pl.when(z > 0)
        def _():
            down(unit, 0).start()

    def hand_on(unit, step):
        @pl.when(jnp.logical_not(corner))
        def _():
            along_x(unit, step).start()
            along_y(unit, step).start()

    def arrived(unit, dist):
        @pl.when(z >= dist)
        def _():
            up(unit, dist - 1).wait_recv()
            if dist < zs - 1:
                @pl.when(z < zs - 1)
                def _():
                    up(unit, dist).start()
            hand_on(unit, zs - dist)

        @pl.when(z + dist < zs)
        def _():
            down(unit, dist - 1).wait_recv()
            if dist < zs - 1:
                @pl.when(z > 0)
                def _():
                    down(unit, dist).start()
            hand_on(unit, dist)

    def frame_copy(buf, which):
        return pltpu.make_async_remote_copy(
            src_ref=buf.at[pl.ds(frames, 2), pl.ds(1, rows)], dst_ref=buf.at[pl.ds(0, 2), pl.ds(1, rows)],
            send_sem=halo_send.at[which, 0], recv_sem=halo_recv.at[which, 0],
            device_id={"group": group + 1}, device_id_type=MESH,
        )

    def row_copy(buf, which, later):
        return pltpu.make_async_remote_copy(
            src_ref=buf.at[:, rows if later else 1], dst_ref=buf.at[:, 0 if later else rows + 1],
            send_sem=halo_send.at[which, 1 + later], recv_sem=halo_recv.at[which, 1 + later],
            device_id={"tile": tile + 1 if later else tile - 1}, device_id_type=MESH,
        )

    def send_frames(buf, which):
        @pl.when(group < groups - 1)
        def _():
            frame_copy(buf, which).start()

    def send_rows(buf, which):
        @pl.when(group > 0)
        def _():
            frame_copy(buf, which).wait_recv()

        @pl.when(tile < tiles - 1)
        def _():
            row_copy(buf, which, 1).start()

        @pl.when(tile > 0)
        def _():
            row_copy(buf, which, 0).start()

    def await_rows(buf, which):
        @pl.when(tile > 0)
        def _():
            row_copy(buf, which, 1).wait_recv()

        @pl.when(tile < tiles - 1)
        def _():
            row_copy(buf, which, 0).wait_recv()

    column = lax.broadcasted_iota(jnp.int32, (across, chans), 0)

    def spread(frame, row, value):
        before = jnp.where(column == 0, 0.0, pltpu.roll(value, 1, 0))
        after = jnp.where(column == across - 1, 0.0, pltpu.roll(value, across - 1, 0))
        cols[frame, row, :, 0:chans] = before.astype(BF16)
        cols[frame, row, :, chans : 2 * chans] = value.astype(BF16)
        cols[frame, row, :, 2 * chans : 3 * chans] = after.astype(BF16)

    def first_columns():
        def step(frame, carry):
            for row in range(rows + 2):
                spread(frame, row, act_slab(lat[frame, row].astype(F32), gain_first[...]))
            return carry
        lax.fori_loop(0, frames + 2, step, 0)

    def second_values():
        def step(frame, carry):
            for row in range(rows):
                hidden = total[frame, row] + bias_first[...]
                sec[frame + 2, row + 1] = act_slab(hidden, gain_second[...]).astype(BF16)
            return carry
        lax.fori_loop(0, frames, step, 0)
        total[...] = jnp.zeros_like(total)

    def second_columns():
        def step(frame, carry):
            for row in range(rows + 2):
                spread(frame, row, sec[frame, row].astype(F32))
            return carry
        lax.fori_loop(0, frames + 2, step, 0)

    def multiply(unit):
        step_t = unit % 3

        def step(step_r, carry):
            window = cols[pl.ds(step_t, frames), pl.ds(step_r, rows)].reshape(-1, 3 * chans)
            weight = taps_all[3 * unit + step_r].reshape(3 * chans, chans)
            added = jnp.dot(window, weight, preferred_element_type=F32)
            total[...] += added.reshape(frames, rows, across, chans)
            return carry
        lax.fori_loop(0, 3, step, 0)

    load(0).wait()
    own(0)
    lat_copy.wait()
    send_frames(lat, 0)
    for unit in range(1, UNITS):
        load(unit).wait()

    def stage(index, lag, body):
        unit = index - lag

        @pl.when((unit >= 0) & (unit < UNITS))
        def _():
            body(unit)

    def direct(unit):
        for step in range(1, zs):
            @pl.when(tile != 2)
            def _():
                along_x(unit, step).wait_recv()

            @pl.when(tile != 1)
            def _():
                along_y(unit, step).wait_recv()

            @pl.when(corner)
            def _():
                along_x(unit, step).start()
                along_y(unit, step).start()

    def forwarded(unit):
        for step in range(1, zs):
            @pl.when(tile == 2)
            def _():
                along_x(unit, step).wait_recv()

            @pl.when(tile == 1)
            def _():
                along_y(unit, step).wait_recv()
        across_cores(unit).start()

    def compute(unit):
        across_cores(unit).wait_recv()
        multiply(unit)

    lag = zs + 1
    def turn(index, carry):
        stage(index, -1, own)
        for dist in range(1, zs):
            stage(index, dist - 1, lambda unit: arrived(unit, dist))

        @pl.when(index == 0)
        def _():
            send_rows(lat, 0)

        @pl.when(index == 2)
        def _():
            await_rows(lat, 0)
            first_columns()

        @pl.when(index == lag + 3)
        def _():
            send_rows(sec, 1)

        stage(index, zs - 1, direct)
        stage(index, zs, forwarded)

        @pl.when(index == lag + 3)
        def _():
            await_rows(sec, 1)
            second_columns()

        stage(index, lag, compute)

        @pl.when(index == lag + 2)
        def _():
            second_values()
            send_frames(sec, 1)
        return carry

    lax.fori_loop(0, UNITS + lag, turn, 0)

    def finish(frame, carry):
        for row in range(rows):
            value = lat[frame + 2, row + 1].astype(F32) + total[frame, row] + bias_second[...]
            out[frame, row] = value.astype(BF16)
        return carry
    lax.fori_loop(0, frames, finish, 0)

    def drain(unit, carry):
        for dist in range(zs - 1):
            @pl.when((z >= dist) & (z < zs - 1))
            def _():
                up(unit, dist).wait_send()

            @pl.when((z + dist < zs) & (z > 0))
            def _():
                down(unit, dist).wait_send()
        for step in range(1, zs):
            along_x(unit, step).wait_send()
            along_y(unit, step).wait_send()
        across_cores(unit).wait_send()
        return carry
    lax.fori_loop(0, UNITS, drain, 0)
    for which, buf in enumerate((lat, sec)):
        @pl.when(group < groups - 1)
        def _():
            frame_copy(buf, which).wait_send()

        @pl.when(tile < tiles - 1)
        def _():
            row_copy(buf, which, 1).wait_send()

        @pl.when(tile > 0)
        def _():
            row_copy(buf, which, 0).wait_send()


def fused_local(latent, gain_first, weight_first, bias_first, gain_second, weight_second, bias_second):
    frames, rows, across, chans = latent.shape
    depth, zs = weight_first.shape[2], lax.axis_size("group") // 2
    line = lambda values: values.reshape(1, chans)
    flat = lambda weight: weight.reshape(9, depth, chans)
    vmem, anywhere = pl.BlockSpec(memory_space=pltpu.VMEM), pl.BlockSpec(memory_space=pl.ANY)
    return pl.pallas_call(
        fused,
        out_shape=jax.ShapeDtypeStruct(latent.shape, BF16),
        in_specs=[anywhere, vmem, anywhere, vmem, vmem, anywhere, vmem],
        out_specs=vmem,
        scratch_shapes=[
            pltpu.VMEM((18, zs, 2, depth, chans), BF16),
            pltpu.VMEM((frames + 2, rows + 2, across, chans), BF16),
            pltpu.VMEM((frames + 2, rows + 2, across, chans), BF16),
            pltpu.VMEM((frames + 2, rows + 2, across, 3 * chans), BF16),
            pltpu.VMEM((frames, rows, across, chans), F32),
            pltpu.SemaphoreType.DMA((UNITS,)),
            pltpu.SemaphoreType.DMA,
            pltpu.SemaphoreType.DMA((UNITS, 2, zs - 1)),
            pltpu.SemaphoreType.DMA((UNITS, 2, zs - 1)),
            pltpu.SemaphoreType.DMA((UNITS, 2, zs - 1)),
            pltpu.SemaphoreType.DMA((UNITS, 2, zs - 1)),
            pltpu.SemaphoreType.DMA((UNITS,)),
            pltpu.SemaphoreType.DMA((UNITS,)),
            pltpu.SemaphoreType.DMA((2, 3)),
            pltpu.SemaphoreType.DMA((2, 3)),
        ],
        compiler_params=pltpu.CompilerParams(
            collective_id=0, has_side_effects=True, vmem_limit_bytes=52 * 1024 * 1024
        ),
        cost_estimate=pl.CostEstimate(
            flops=4 * frames * rows * across * 27 * chans * chans,
            bytes_accessed=4 * 9 * depth * chans + 4 * frames * rows * across * chans,
            transcendentals=0,
        ),
    )(latent, line(gain_first), flat(weight_first), line(bias_first), line(gain_second), flat(weight_second), line(bias_second))


def solution(mesh):
    small = mesh.shape["tile"] == 4 and mesh.shape["group"] == 8
    return jax.shard_map(
        fused_local if small else local,
        mesh=mesh,
        in_specs=(
            P(("cand", "group"), "tile", None, None),
            P(),
            P(None, None, "group", None),
            P(),
            P(),
            P(None, None, "group", None),
            P(),
        ),
        out_specs=P(("cand", "group"), "tile", None, None),
        check_vma=False,
    )
```

```python
import jax
import jax.numpy as jnp
from jax import lax
from jax.experimental import pallas as pl
from jax.experimental.pallas import tpu as pltpu
from jax.sharding import PartitionSpec as P


def shifted(value, axis, steps):
    count = lax.axis_size(axis)
    first, last = (max(0, -steps), min(count, count - steps))
    return lax.ppermute(value, axis, [(source, source + steps) for source in range(first, last)])


def with_halo(array, sides, width):
    for axis, dim in sides:
        size, length = (lax.axis_size(axis), array.shape[dim])
        up = [(i, (i + 1) % size) for i in range(size - 1)]
        down = [(j, i) for i, j in up]
        last = lax.slice_in_dim(array, length - width, length, axis=dim)
        first = lax.slice_in_dim(array, 0, width, axis=dim)
        before = lax.ppermute(last, axis, up)
        after = lax.ppermute(first, axis, down)
        array = jnp.concatenate([before, array, after], axis=dim)
    return array


def activate(values, gain):
    wide = values.astype(jnp.float32)
    scaled = wide * lax.rsqrt(jnp.mean(wide * wide, axis=-1, keepdims=True) + 1e-06) * gain
    return jax.nn.silu(scaled)


def widen(grown):
    across = grown.shape[2]
    padded = jnp.pad(grown, ((0, 0), (0, 0), (1, 1), (0, 0)))
    return jnp.concatenate([padded[:, :, k : k + across] for k in range(3)], axis=-1)


def taps(joined, piece):
    count = joined.shape[0] - 2
    tall = joined.shape[1] - 2
    across = joined.shape[2]
    inner = piece.shape[2]
    total = jnp.zeros((count * tall * across, piece.shape[3]), jnp.float32)
    for step_t in range(3):
        for step_r in range(3):
            window = joined[step_t : step_t + count, step_r : step_r + tall].reshape(-1, inner)
            total = total + jnp.dot(
                window, piece[step_t, step_r], preferred_element_type=jnp.float32
            )
    return total.reshape(count, tall, across, piece.shape[3])


def local(latent, gain_first, weight_first, bias_first, gain_second, weight_second, bias_second):
    frames, rows, width, chans = latent.shape
    depth = 1
    first = activate(latent, gain_first).astype(jnp.bfloat16)
    earlier = shifted(first[frames - 2 :], "group", 1)
    stacked = jnp.concatenate([earlier, first], axis=0)
    grown = with_halo(stacked, (("tile", 1),), depth)
    joined_first = widen(grown)
    hidden = (
        taps(joined_first, lax.all_gather(weight_first, "group", axis=2, tiled=True)) + bias_first
    )
    second = activate(hidden, gain_second)
    second = second.astype(jnp.bfloat16)
    later = shifted(second[frames - 2 :], "group", 1)
    second = jnp.concatenate([later, second], axis=0)
    second = with_halo(second, (("tile", 1),), 1)
    joined_second = widen(second)
    branch = taps(joined_second, lax.all_gather(weight_second, "group", axis=2, tiled=True))
    result = latent.astype(jnp.float32) + branch + bias_second
    return result.astype(jnp.bfloat16)


BF16, F32 = jnp.bfloat16, jnp.float32
MESH = pl.DeviceIdType.MESH
UNITS = 18
AHEAD = 3
LAG = 2


def act_slab(wide, gain):
    square = jnp.sum(wide * wide, axis=-1, keepdims=True) * (1.0 / wide.shape[-1])
    scaled = wide * lax.rsqrt(square + 1e-06) * gain
    return scaled / (1.0 + jnp.exp(-scaled))


def fused(
    latent, gain_first_in, weight_first, bias_first_in, gain_second_in, weight_second, bias_second_in, out,
    taps_all, lat, sec, cols, total, gain_first, bias_first, gain_second, bias_second,
    load_sem, lat_sem, line_sem, z_send, z_recv, xy_send, xy_recv, core_send, core_recv, halo_send, halo_recv,
):
    tile, group = lax.axis_index("tile"), lax.axis_index("group")
    tiles, groups = lax.axis_size("tile"), lax.axis_size("group")
    y, x = tile // 2, tile % 2
    z, core = group // 2, group % 2
    zs = groups // 2
    frames, rows, across, chans = latent.shape
    x_tile, y_tile = 2 * y + (1 - x), 2 * (1 - y) + x
    z_part = x + 2 * y - 3 * x * y
    x_part = x + 2 * y - 2 * x * y
    y_part = x + 2 * y - x * y
    corner = (x + y) == 2

    lat[...] = jnp.zeros_like(lat)
    sec[...] = jnp.zeros_like(sec)
    total[...] = jnp.zeros_like(total)


    def load(at):
        source, low, count, start = ((weight_first, 0, 1, 0), (weight_first, 1, 8, 1), (weight_second, 0, 9, 9))[at]
        return pltpu.make_async_copy(
            source.at[pl.ds(low, count)],
            taps_all.at[pl.ds(start, count), z, pl.ds(3 * core, 3)],
            load_sem.at[at],
        )

    line_copies = [
        pltpu.make_async_copy(source, line, line_sem.at[at])
        for at, (source, line) in enumerate(
            (
                (gain_first_in, gain_first),
                (bias_first_in, bias_first),
                (gain_second_in, gain_second),
                (bias_second_in, bias_second),
            )
        )
    ]

    lat_copy = pltpu.make_async_copy(
        latent, lat.at[pl.ds(2, frames), pl.ds(1, rows)], lat_sem
    )
    load(0).start()
    lat_copy.start()
    load(1).start()
    load(2).start()
    for copy in line_copies:
        copy.start()

    barrier = pltpu.get_barrier_semaphore()
    partners = [
        ({"group": group + 2}, z < zs - 1),
        ({"group": group - 2}, z > 0),
        ({"group": group + 1}, group < groups - 1),
        ({"group": group - 1}, group > 0),
        ({"tile": tile + 1}, tile < tiles - 1),
        ({"tile": tile - 1}, tile > 0),
        ({"tile": x_tile}, None),
        ({"tile": y_tile}, None),
    ]
    expected = 0
    for where, there in partners:
        if there is None:
            pl.semaphore_signal(barrier, inc=1, device_id=where, device_id_type=MESH)
            expected = expected + 1
        else:
            @pl.when(there)
            def _():
                pl.semaphore_signal(barrier, inc=1, device_id=where, device_id_type=MESH)
            expected = expected + there.astype(jnp.int32)
    pl.semaphore_wait(barrier, expected)

    def piece(unit, part, origin, where, send, recv):
        block = taps_all.at[unit, origin, 3 * core + part]
        return pltpu.make_async_remote_copy(
            src_ref=block, dst_ref=block, send_sem=send, recv_sem=recv,
            device_id=where, device_id_type=MESH,
        )

    def up(unit, dist):
        return piece(unit, z_part, z - dist, {"group": group + 2}, z_send.at[unit], z_recv.at[unit, 0, dist])

    def down(unit, dist):
        return piece(unit, z_part, z + dist, {"group": group - 2}, z_send.at[unit], z_recv.at[unit, 1, dist])

    def along_x(unit, step):
        return piece(unit, x_part, (z + step) % zs, {"tile": x_tile}, xy_send.at[unit], xy_recv.at[unit, 0])

    def along_y(unit, step):
        return piece(unit, y_part, (z + step) % zs, {"tile": y_tile}, xy_send.at[unit], xy_recv.at[unit, 1])

    def wait_pieces(count, sem):
        block = taps_all.at[0, 0, pl.ds(0, count)]
        pltpu.make_async_copy(block, block, sem).wait()

    def across_cores(unit):
        block = taps_all.at[unit, :, pl.ds(3 * core, 3)]
        return pltpu.make_async_remote_copy(
            src_ref=block, dst_ref=block, send_sem=core_send.at[unit], recv_sem=core_recv.at[unit],
            device_id={"group": 2 * z + (1 - core)}, device_id_type=MESH,
        )

    def own(unit):
        @pl.when(z < zs - 1)
        def _():
            up(unit, 0).start()

        @pl.when(z > 0)
        def _():
            down(unit, 0).start()

    def hand_on(unit, step):
        @pl.when(jnp.logical_not(corner))
        def _():
            along_x(unit, step).start()
            along_y(unit, step).start()

    def arrived(unit, dist):
        @pl.when(z >= dist)
        def _():
            up(unit, dist - 1).wait_recv()
            if dist < zs - 1:
                @pl.when(z < zs - 1)
                def _():
                    up(unit, dist).start()
            hand_on(unit, zs - dist)

        @pl.when(z + dist < zs)
        def _():
            down(unit, dist - 1).wait_recv()
            if dist < zs - 1:
                @pl.when(z > 0)
                def _():
                    down(unit, dist).start()
            hand_on(unit, dist)

    def frame_copy(buf, which):
        return pltpu.make_async_remote_copy(
            src_ref=buf.at[pl.ds(frames, 2), pl.ds(1, rows)], dst_ref=buf.at[pl.ds(0, 2), pl.ds(1, rows)],
            send_sem=halo_send.at[which, 0], recv_sem=halo_recv.at[which, 0],
            device_id={"group": group + 1}, device_id_type=MESH,
        )

    def row_copy(buf, which, later):
        return pltpu.make_async_remote_copy(
            src_ref=buf.at[:, rows if later else 1], dst_ref=buf.at[:, 0 if later else rows + 1],
            send_sem=halo_send.at[which, 1 + later], recv_sem=halo_recv.at[which, 1 + later],
            device_id={"tile": tile + 1 if later else tile - 1}, device_id_type=MESH,
        )

    def send_frames(buf, which):
        @pl.when(group < groups - 1)
        def _():
            frame_copy(buf, which).start()

    def send_rows(buf, which):
        @pl.when(group > 0)
        def _():
            frame_copy(buf, which).wait_recv()

        @pl.when(tile < tiles - 1)
        def _():
            row_copy(buf, which, 1).start()

        @pl.when(tile > 0)
        def _():
            row_copy(buf, which, 0).start()

    def await_rows(buf, which):
        @pl.when(tile > 0)
        def _():
            row_copy(buf, which, 1).wait_recv()

        @pl.when(tile < tiles - 1)
        def _():
            row_copy(buf, which, 0).wait_recv()

    column = lax.broadcasted_iota(jnp.int32, (across, chans), 0)

    def spread(frame, row, value):
        before = jnp.where(column == 0, 0.0, pltpu.roll(value, 1, 0))
        after = jnp.where(column == across - 1, 0.0, pltpu.roll(value, across - 1, 0))
        cols[frame, row, :, 0:chans] = before.astype(BF16)
        cols[frame, row, :, chans : 2 * chans] = value.astype(BF16)
        cols[frame, row, :, 2 * chans : 3 * chans] = after.astype(BF16)

    def first_columns():
        def step(frame, carry):
            for row in range(rows + 2):
                spread(frame, row, act_slab(lat[frame, row].astype(F32), gain_first[...][None]))
            return carry
        lax.fori_loop(0, frames + 2, step, 0)

    def second_values():
        def step(frame, carry):
            for row in range(rows):
                hidden = total[frame, row] + bias_first[...][None]
                sec[frame + 2, row + 1] = act_slab(hidden, gain_second[...][None]).astype(BF16)
            return carry
        lax.fori_loop(0, frames, step, 0)
        total[...] = jnp.zeros_like(total)

    def second_columns():
        def step(frame, carry):
            for row in range(rows + 2):
                spread(frame, row, sec[frame, row].astype(F32))
            return carry
        lax.fori_loop(0, frames + 2, step, 0)

    def multiply(unit):
        step_t, step_r = (unit % 9) // 3, unit % 3
        window = cols[pl.ds(step_t, frames), pl.ds(step_r, rows)].reshape(-1, 3 * chans)
        weight = taps_all[unit].reshape(3 * chans, chans)
        added = jnp.dot(window, weight, preferred_element_type=F32)
        total[...] += added.reshape(frames, rows, across, chans)

    load(0).wait()
    own(0)
    lat_copy.wait()
    load(1).wait()
    for unit in range(1, AHEAD):
        own(unit)
    send_frames(lat, 0)
    load(2).wait()
    for copy in line_copies:
        copy.wait()

    def stage(index, lag, body):
        unit = index - lag

        @pl.when((unit >= 0) & (unit < UNITS))
        def _():
            body(unit)

    def direct(unit):
        @pl.when(tile != 2)
        def _():
            wait_pieces(3, xy_recv.at[unit, 0])

        @pl.when(tile != 1)
        def _():
            wait_pieces(3, xy_recv.at[unit, 1])

        @pl.when(corner)
        def _():
            for step in range(1, zs):
                along_x(unit, step).start()
                along_y(unit, step).start()

    def forwarded(unit):
        @pl.when(tile == 2)
        def _():
            wait_pieces(3, xy_recv.at[unit, 0])

        @pl.when(tile == 1)
        def _():
            wait_pieces(3, xy_recv.at[unit, 1])
        across_cores(unit).start()

    def compute(unit, carry):
        across_cores(unit).wait_recv()
        multiply(unit)
        return carry

    def drain(unit):
        @pl.when((z > 0) & (z < zs - 1))
        def _():
            wait_pieces(zs + 1, z_send.at[unit])

        @pl.when((z == 0) | (z == zs - 1))
        def _():
            wait_pieces(1, z_send.at[unit])
        wait_pieces(2 * zs - 2, xy_send.at[unit])
        across_cores(unit).wait_send()

    half = UNITS // 2
    direct_lag = LAG * (zs - 1)
    forward_lag = direct_lag + LAG
    first_lag = forward_lag + LAG
    middle = half - 1 + first_lag
    drain_lag = first_lag + 4
    turns = UNITS + forward_lag + 1

    def done_by(index):
        first = jnp.clip(index - first_lag + 1, 0, half)
        second = jnp.clip(jnp.minimum(2 * (index - middle - 2), index - forward_lag - half), 0, half)
        return first + second

    def turn(index, carry):
        stage(index, -AHEAD, own)
        for dist in range(1, zs):
            stage(index, LAG * (dist - 1), lambda unit: arrived(unit, dist))
        stage(index, direct_lag, direct)
        stage(index, forward_lag, forwarded)
        stage(index, drain_lag, drain)
        lax.fori_loop(done_by(index - 1), done_by(index), compute, 0)

        @pl.when(index == 1)
        def _():
            send_rows(lat, 0)

        @pl.when(index == 3)
        def _():
            await_rows(lat, 0)
            first_columns()

        @pl.when(index == middle)
        def _():
            second_values()
            send_frames(sec, 1)

        @pl.when(index == middle + 1)
        def _():
            send_rows(sec, 1)

        @pl.when(index == middle + 2)
        def _():
            await_rows(sec, 1)
            second_columns()
        return carry

    lax.fori_loop(0, turns, turn, 0)

    def finish(frame, carry):
        for row in range(rows):
            value = lat[frame + 2, row + 1].astype(F32) + total[frame, row] + bias_second[...][None]
            out[frame, row] = value.astype(BF16)
        return carry
    lax.fori_loop(0, frames, finish, 0)

    def drain_rest(unit, carry):
        drain(unit)
        return carry
    lax.fori_loop(turns - drain_lag, UNITS, drain_rest, 0)
    for which, buf in enumerate((lat, sec)):
        @pl.when(group < groups - 1)
        def _():
            frame_copy(buf, which).wait_send()

        @pl.when(tile < tiles - 1)
        def _():
            row_copy(buf, which, 1).wait_send()

        @pl.when(tile > 0)
        def _():
            row_copy(buf, which, 0).wait_send()


def fused_local(latent, gain_first, weight_first, bias_first, gain_second, weight_second, bias_second):
    frames, rows, across, chans = latent.shape
    depth, zs = weight_first.shape[2], lax.axis_size("group") // 2
    flat = lambda weight: weight.reshape(9, 3, depth // 3, chans)
    anywhere = pl.BlockSpec(memory_space=pl.ANY)
    return pl.pallas_call(
        fused,
        out_shape=jax.ShapeDtypeStruct(latent.shape, BF16),
        in_specs=[anywhere] * 7,
        out_specs=pl.BlockSpec(memory_space=pltpu.VMEM),
        scratch_shapes=[
            pltpu.VMEM((UNITS, zs, 6, depth // 3, chans), BF16),
            pltpu.VMEM((frames + 2, rows + 2, across, chans), BF16),
            pltpu.VMEM((frames + 2, rows + 2, across, chans), BF16),
            pltpu.VMEM((frames + 2, rows + 2, across, 3 * chans), BF16),
            pltpu.VMEM((frames, rows, across, chans), F32),
            *[pltpu.VMEM((chans,), F32)] * 4,
            pltpu.SemaphoreType.DMA((3,)),
            pltpu.SemaphoreType.DMA,
            pltpu.SemaphoreType.DMA((4,)),
            pltpu.SemaphoreType.DMA((UNITS,)),
            pltpu.SemaphoreType.DMA((UNITS, 2, zs - 1)),
            pltpu.SemaphoreType.DMA((UNITS,)),
            pltpu.SemaphoreType.DMA((UNITS, 2)),
            pltpu.SemaphoreType.DMA((UNITS,)),
            pltpu.SemaphoreType.DMA((UNITS,)),
            pltpu.SemaphoreType.DMA((2, 3)),
            pltpu.SemaphoreType.DMA((2, 3)),
        ],
        compiler_params=pltpu.CompilerParams(
            collective_id=0, has_side_effects=True, vmem_limit_bytes=60 * 1024 * 1024
        ),
        cost_estimate=pl.CostEstimate(
            flops=4 * frames * rows * across * 27 * chans * chans,
            bytes_accessed=4 * 9 * depth * chans + 4 * frames * rows * across * chans,
            transcendentals=0,
        ),
    )(latent, gain_first, flat(weight_first), bias_first, gain_second, flat(weight_second), bias_second)


def solution(mesh):
    small = mesh.shape["tile"] == 4 and mesh.shape["group"] == 8
    return jax.shard_map(
        fused_local if small else local,
        mesh=mesh,
        in_specs=(
            P(("cand", "group"), "tile", None, None),
            P(),
            P(None, None, "group", None),
            P(),
            P(),
            P(None, None, "group", None),
            P(),
        ),
        out_specs=P(("cand", "group"), "tile", None, None),
        check_vma=False,
    )
```

```python
import jax
import jax.numpy as jnp
from jax import lax
from jax.experimental import pallas as pl
from jax.experimental.pallas import tpu as pltpu
from jax.sharding import PartitionSpec as P


def shifted(value, axis, steps):
    count = lax.axis_size(axis)
    first, last = (max(0, -steps), min(count, count - steps))
    return lax.ppermute(value, axis, [(source, source + steps) for source in range(first, last)])


def with_halo(array, sides, width):
    for axis, dim in sides:
        size, length = (lax.axis_size(axis), array.shape[dim])
        up = [(i, (i + 1) % size) for i in range(size - 1)]
        down = [(j, i) for i, j in up]
        last = lax.slice_in_dim(array, length - width, length, axis=dim)
        first = lax.slice_in_dim(array, 0, width, axis=dim)
        before = lax.ppermute(last, axis, up)
        after = lax.ppermute(first, axis, down)
        array = jnp.concatenate([before, array, after], axis=dim)
    return array


def activate(values, gain):
    wide = values.astype(jnp.float32)
    scaled = wide * lax.rsqrt(jnp.mean(wide * wide, axis=-1, keepdims=True) + 1e-06) * gain
    return jax.nn.silu(scaled)


def widen(grown):
    across = grown.shape[2]
    padded = jnp.pad(grown, ((0, 0), (0, 0), (1, 1), (0, 0)))
    return jnp.concatenate([padded[:, :, k : k + across] for k in range(3)], axis=-1)


def taps(joined, piece):
    count = joined.shape[0] - 2
    tall = joined.shape[1] - 2
    across = joined.shape[2]
    inner = piece.shape[2]
    total = jnp.zeros((count * tall * across, piece.shape[3]), jnp.float32)
    for step_t in range(3):
        for step_r in range(3):
            window = joined[step_t : step_t + count, step_r : step_r + tall].reshape(-1, inner)
            total = total + jnp.dot(
                window, piece[step_t, step_r], preferred_element_type=jnp.float32
            )
    return total.reshape(count, tall, across, piece.shape[3])


def local(latent, gain_first, weight_first, bias_first, gain_second, weight_second, bias_second):
    frames, rows, width, chans = latent.shape
    depth = 1
    first = activate(latent, gain_first).astype(jnp.bfloat16)
    earlier = shifted(first[frames - 2 :], "group", 1)
    stacked = jnp.concatenate([earlier, first], axis=0)
    grown = with_halo(stacked, (("tile", 1),), depth)
    joined_first = widen(grown)
    hidden = (
        taps(joined_first, lax.all_gather(weight_first, "group", axis=2, tiled=True)) + bias_first
    )
    second = activate(hidden, gain_second)
    second = second.astype(jnp.bfloat16)
    later = shifted(second[frames - 2 :], "group", 1)
    second = jnp.concatenate([later, second], axis=0)
    second = with_halo(second, (("tile", 1),), 1)
    joined_second = widen(second)
    branch = taps(joined_second, lax.all_gather(weight_second, "group", axis=2, tiled=True))
    result = latent.astype(jnp.float32) + branch + bias_second
    return result.astype(jnp.bfloat16)


BF16, F32 = jnp.bfloat16, jnp.float32
MESH = pl.DeviceIdType.MESH
UNITS = 18
AHEAD = 6
LAG = 3


def act_slab(wide, gain):
    square = jnp.sum(wide * wide, axis=-1, keepdims=True) * (1.0 / wide.shape[-1])
    scaled = wide * lax.rsqrt(square + 1e-06) * gain
    return scaled / (1.0 + jnp.exp(-scaled))


def fused(
    latent, gain_first_in, weight_first, bias_first_in, gain_second_in, weight_second, bias_second_in, out,
    taps_all, lat, sec, cols, total, gain_first, bias_first, gain_second, bias_second,
    load_sem, lat_sem, line_sem, z_send, z_recv, xy_send, xy_recv, core_send, core_recv, halo_send, halo_recv,
):
    tile, group = lax.axis_index("tile"), lax.axis_index("group")
    tiles, groups = lax.axis_size("tile"), lax.axis_size("group")
    y, x = tile // 2, tile % 2
    z, core = group // 2, group % 2
    zs = groups // 2
    frames, rows, across, chans = latent.shape
    x_tile, y_tile = 2 * y + (1 - x), 2 * (1 - y) + x
    z_part = x + 2 * y - 3 * x * y
    x_part = x + 2 * y - 2 * x * y
    y_part = x + 2 * y - x * y
    corner = (x + y) == 2

    lat[...] = jnp.zeros_like(lat)
    sec[...] = jnp.zeros_like(sec)
    total[...] = jnp.zeros_like(total)


    def load(at):
        source, low, count, start = ((weight_first, 0, 1, 0), (weight_first, 1, 8, 1), (weight_second, 0, 9, 9))[at]
        return pltpu.make_async_copy(
            source.at[pl.ds(low, count)],
            taps_all.at[pl.ds(start, count), z, pl.ds(3 * core, 3)],
            load_sem.at[at],
        )

    line_copies = [
        pltpu.make_async_copy(source, line, line_sem.at[at])
        for at, (source, line) in enumerate(
            (
                (gain_first_in, gain_first),
                (bias_first_in, bias_first),
                (gain_second_in, gain_second),
                (bias_second_in, bias_second),
            )
        )
    ]

    lat_copy = pltpu.make_async_copy(
        latent, lat.at[pl.ds(2, frames), pl.ds(1, rows)], lat_sem
    )
    load(0).start()
    lat_copy.start()
    load(1).start()
    load(2).start()
    for copy in line_copies:
        copy.start()

    barrier = pltpu.get_barrier_semaphore()
    partners = [
        ({"group": group + 2}, z < zs - 1),
        ({"group": group - 2}, z > 0),
        ({"group": group + 1}, group < groups - 1),
        ({"group": group - 1}, group > 0),
        ({"tile": tile + 1}, tile < tiles - 1),
        ({"tile": tile - 1}, tile > 0),
        ({"tile": x_tile}, None),
        ({"tile": y_tile}, None),
    ]
    expected = 0
    for where, there in partners:
        if there is None:
            pl.semaphore_signal(barrier, inc=1, device_id=where, device_id_type=MESH)
            expected = expected + 1
        else:
            @pl.when(there)
            def _():
                pl.semaphore_signal(barrier, inc=1, device_id=where, device_id_type=MESH)
            expected = expected + there.astype(jnp.int32)
    pl.semaphore_wait(barrier, expected)

    def piece(unit, part, origin, where, send, recv):
        block = taps_all.at[unit, origin, 3 * core + part]
        return pltpu.make_async_remote_copy(
            src_ref=block, dst_ref=block, send_sem=send, recv_sem=recv,
            device_id=where, device_id_type=MESH,
        )

    def up(unit, dist):
        return piece(unit, z_part, z - dist, {"group": group + 2}, z_send.at[unit], z_recv.at[unit, 0, dist])

    def down(unit, dist):
        return piece(unit, z_part, z + dist, {"group": group - 2}, z_send.at[unit], z_recv.at[unit, 1, dist])

    def along_x(unit, step):
        return piece(unit, x_part, (z + step) % zs, {"tile": x_tile}, xy_send.at[unit], xy_recv.at[unit, 0])

    def along_y(unit, step):
        return piece(unit, y_part, (z + step) % zs, {"tile": y_tile}, xy_send.at[unit], xy_recv.at[unit, 1])

    def wait_pieces(count, sem):
        block = taps_all.at[0, 0, pl.ds(0, count)]
        pltpu.make_async_copy(block, block, sem).wait()

    def across_cores(unit):
        block = taps_all.at[unit, :, pl.ds(3 * core, 3)]
        return pltpu.make_async_remote_copy(
            src_ref=block, dst_ref=block, send_sem=core_send.at[unit], recv_sem=core_recv.at[unit],
            device_id={"group": 2 * z + (1 - core)}, device_id_type=MESH,
        )

    def own(unit):
        @pl.when(z < zs - 1)
        def _():
            up(unit, 0).start()

        @pl.when(z > 0)
        def _():
            down(unit, 0).start()

    def hand_on(unit, step):
        @pl.when(jnp.logical_not(corner))
        def _():
            along_x(unit, step).start()
            along_y(unit, step).start()

    def arrived(unit, dist):
        @pl.when(z >= dist)
        def _():
            up(unit, dist - 1).wait_recv()
            if dist < zs - 1:
                @pl.when(z < zs - 1)
                def _():
                    up(unit, dist).start()
            hand_on(unit, zs - dist)

        @pl.when(z + dist < zs)
        def _():
            down(unit, dist - 1).wait_recv()
            if dist < zs - 1:
                @pl.when(z > 0)
                def _():
                    down(unit, dist).start()
            hand_on(unit, dist)

    def frame_copy(buf, which):
        return pltpu.make_async_remote_copy(
            src_ref=buf.at[pl.ds(frames, 2), pl.ds(1, rows)], dst_ref=buf.at[pl.ds(0, 2), pl.ds(1, rows)],
            send_sem=halo_send.at[which, 0], recv_sem=halo_recv.at[which, 0],
            device_id={"group": group + 1}, device_id_type=MESH,
        )

    def row_copy(buf, which, later):
        return pltpu.make_async_remote_copy(
            src_ref=buf.at[:, rows if later else 1], dst_ref=buf.at[:, 0 if later else rows + 1],
            send_sem=halo_send.at[which, 1 + later], recv_sem=halo_recv.at[which, 1 + later],
            device_id={"tile": tile + 1 if later else tile - 1}, device_id_type=MESH,
        )

    def send_frames(buf, which):
        @pl.when(group < groups - 1)
        def _():
            frame_copy(buf, which).start()

    def send_rows(buf, which):
        @pl.when(group > 0)
        def _():
            frame_copy(buf, which).wait_recv()

        @pl.when(tile < tiles - 1)
        def _():
            row_copy(buf, which, 1).start()

        @pl.when(tile > 0)
        def _():
            row_copy(buf, which, 0).start()

    def await_rows(buf, which):
        @pl.when(tile > 0)
        def _():
            row_copy(buf, which, 1).wait_recv()

        @pl.when(tile < tiles - 1)
        def _():
            row_copy(buf, which, 0).wait_recv()

    column = lax.broadcasted_iota(jnp.int32, (across, chans), 0)

    def spread(frame, row, value):
        before = jnp.where(column == 0, 0.0, pltpu.roll(value, 1, 0))
        after = jnp.where(column == across - 1, 0.0, pltpu.roll(value, across - 1, 0))
        cols[frame, row, :, 0:chans] = before.astype(BF16)
        cols[frame, row, :, chans : 2 * chans] = value.astype(BF16)
        cols[frame, row, :, 2 * chans : 3 * chans] = after.astype(BF16)

    def first_columns():
        def step(frame, carry):
            for row in range(rows + 2):
                spread(frame, row, act_slab(lat[frame, row].astype(F32), gain_first[...][None]))
            return carry
        lax.fori_loop(0, frames + 2, step, 0)

    def second_values():
        def step(frame, carry):
            for row in range(rows):
                hidden = total[frame, row] + bias_first[...][None]
                sec[frame + 2, row + 1] = act_slab(hidden, gain_second[...][None]).astype(BF16)
            return carry
        lax.fori_loop(0, frames, step, 0)
        total[...] = jnp.zeros_like(total)

    def second_columns():
        def step(frame, carry):
            for row in range(rows + 2):
                spread(frame, row, sec[frame, row].astype(F32))
            return carry
        lax.fori_loop(0, frames + 2, step, 0)

    def multiply(unit):
        step_t, step_r = (unit % 9) // 3, unit % 3
        window = cols[pl.ds(step_t, frames), pl.ds(step_r, rows)].reshape(-1, 3 * chans)
        weight = taps_all[unit].reshape(3 * chans, chans)
        added = jnp.dot(window, weight, preferred_element_type=F32)
        total[...] += added.reshape(frames, rows, across, chans)

    load(0).wait()
    own(0)
    lat_copy.wait()
    load(1).wait()
    for unit in range(1, AHEAD):
        own(unit)
    send_frames(lat, 0)
    load(2).wait()
    for copy in line_copies:
        copy.wait()

    def stage(index, lag, body):
        unit = index - lag

        @pl.when((unit >= 0) & (unit < UNITS))
        def _():
            body(unit)

    def direct(unit):
        @pl.when(tile != 2)
        def _():
            wait_pieces(3, xy_recv.at[unit, 0])

        @pl.when(tile != 1)
        def _():
            wait_pieces(3, xy_recv.at[unit, 1])

        @pl.when(corner)
        def _():
            for step in range(1, zs):
                along_x(unit, step).start()
                along_y(unit, step).start()

    def forwarded(unit):
        @pl.when(tile == 2)
        def _():
            wait_pieces(3, xy_recv.at[unit, 0])

        @pl.when(tile == 1)
        def _():
            wait_pieces(3, xy_recv.at[unit, 1])
        across_cores(unit).start()

    def compute(unit, carry):
        across_cores(unit).wait_recv()
        multiply(unit)
        return carry

    def drain(unit):
        @pl.when((z > 0) & (z < zs - 1))
        def _():
            wait_pieces(zs + 1, z_send.at[unit])

        @pl.when((z == 0) | (z == zs - 1))
        def _():
            wait_pieces(1, z_send.at[unit])
        wait_pieces(2 * zs - 2, xy_send.at[unit])
        across_cores(unit).wait_send()

    half = UNITS // 2
    direct_lag = LAG * (zs - 1)
    forward_lag = direct_lag + LAG
    first_lag = forward_lag + LAG
    middle = half - 1 + first_lag
    drain_lag = first_lag + 4
    turns = UNITS + forward_lag + 1

    def done_by(index):
        first = jnp.clip(index - first_lag + 1, 0, half)
        second = jnp.clip(jnp.minimum(2 * (index - middle - 2), index - forward_lag - half), 0, half)
        return first + second

    def turn(index, carry):
        stage(index, -AHEAD, own)
        for dist in range(1, zs):
            stage(index, LAG * (dist - 1), lambda unit: arrived(unit, dist))
        stage(index, direct_lag, direct)
        stage(index, forward_lag, forwarded)
        stage(index, drain_lag, drain)
        lax.fori_loop(done_by(index - 1), done_by(index), compute, 0)

        @pl.when(index == 1)
        def _():
            send_rows(lat, 0)

        @pl.when(index == 3)
        def _():
            await_rows(lat, 0)
            first_columns()

        @pl.when(index == middle)
        def _():
            second_values()
            send_frames(sec, 1)

        @pl.when(index == middle + 1)
        def _():
            send_rows(sec, 1)

        @pl.when(index == middle + 2)
        def _():
            await_rows(sec, 1)
            second_columns()
        return carry

    lax.fori_loop(0, turns, turn, 0)

    def finish(frame, carry):
        for row in range(rows):
            value = lat[frame + 2, row + 1].astype(F32) + total[frame, row] + bias_second[...][None]
            out[frame, row] = value.astype(BF16)
        return carry
    lax.fori_loop(0, frames, finish, 0)

    def drain_rest(unit, carry):
        drain(unit)
        return carry
    lax.fori_loop(turns - drain_lag, UNITS, drain_rest, 0)
    for which, buf in enumerate((lat, sec)):
        @pl.when(group < groups - 1)
        def _():
            frame_copy(buf, which).wait_send()

        @pl.when(tile < tiles - 1)
        def _():
            row_copy(buf, which, 1).wait_send()

        @pl.when(tile > 0)
        def _():
            row_copy(buf, which, 0).wait_send()


def fused_local(latent, gain_first, weight_first, bias_first, gain_second, weight_second, bias_second):
    frames, rows, across, chans = latent.shape
    depth, zs = weight_first.shape[2], lax.axis_size("group") // 2
    flat = lambda weight: weight.reshape(9, 3, depth // 3, chans)
    anywhere = pl.BlockSpec(memory_space=pl.ANY)
    return pl.pallas_call(
        fused,
        out_shape=jax.ShapeDtypeStruct(latent.shape, BF16),
        in_specs=[anywhere] * 7,
        out_specs=pl.BlockSpec(memory_space=pltpu.VMEM),
        scratch_shapes=[
            pltpu.VMEM((UNITS, zs, 6, depth // 3, chans), BF16),
            pltpu.VMEM((frames + 2, rows + 2, across, chans), BF16),
            pltpu.VMEM((frames + 2, rows + 2, across, chans), BF16),
            pltpu.VMEM((frames + 2, rows + 2, across, 3 * chans), BF16),
            pltpu.VMEM((frames, rows, across, chans), F32),
            *[pltpu.VMEM((chans,), F32)] * 4,
            pltpu.SemaphoreType.DMA((3,)),
            pltpu.SemaphoreType.DMA,
            pltpu.SemaphoreType.DMA((4,)),
            pltpu.SemaphoreType.DMA((UNITS,)),
            pltpu.SemaphoreType.DMA((UNITS, 2, zs - 1)),
            pltpu.SemaphoreType.DMA((UNITS,)),
            pltpu.SemaphoreType.DMA((UNITS, 2)),
            pltpu.SemaphoreType.DMA((UNITS,)),
            pltpu.SemaphoreType.DMA((UNITS,)),
            pltpu.SemaphoreType.DMA((2, 3)),
            pltpu.SemaphoreType.DMA((2, 3)),
        ],
        compiler_params=pltpu.CompilerParams(
            collective_id=0, has_side_effects=True, vmem_limit_bytes=60 * 1024 * 1024
        ),
        cost_estimate=pl.CostEstimate(
            flops=4 * frames * rows * across * 27 * chans * chans,
            bytes_accessed=4 * 9 * depth * chans + 4 * frames * rows * across * chans,
            transcendentals=0,
        ),
    )(latent, gain_first, flat(weight_first), bias_first, gain_second, flat(weight_second), bias_second)


def solution(mesh):
    small = mesh.shape["tile"] == 4 and mesh.shape["group"] == 8
    return jax.shard_map(
        fused_local if small else local,
        mesh=mesh,
        in_specs=(
            P(("cand", "group"), "tile", None, None),
            P(),
            P(None, None, "group", None),
            P(),
            P(),
            P(None, None, "group", None),
            P(),
        ),
        out_specs=P(("cand", "group"), "tile", None, None),
        check_vma=False,
    )
```

```python
import jax
import jax.numpy as jnp
from jax import lax
from jax.experimental import pallas as pl
from jax.experimental.pallas import tpu as pltpu
from jax.sharding import PartitionSpec as P


def shifted(value, axis, steps):
    count = lax.axis_size(axis)
    first, last = (max(0, -steps), min(count, count - steps))
    return lax.ppermute(value, axis, [(source, source + steps) for source in range(first, last)])


def with_halo(array, sides, width):
    for axis, dim in sides:
        size, length = (lax.axis_size(axis), array.shape[dim])
        up = [(i, (i + 1) % size) for i in range(size - 1)]
        down = [(j, i) for i, j in up]
        last = lax.slice_in_dim(array, length - width, length, axis=dim)
        first = lax.slice_in_dim(array, 0, width, axis=dim)
        before = lax.ppermute(last, axis, up)
        after = lax.ppermute(first, axis, down)
        array = jnp.concatenate([before, array, after], axis=dim)
    return array


def activate(values, gain):
    wide = values.astype(jnp.float32)
    scaled = wide * lax.rsqrt(jnp.mean(wide * wide, axis=-1, keepdims=True) + 1e-06) * gain
    return jax.nn.silu(scaled)


def widen(grown):
    across = grown.shape[2]
    padded = jnp.pad(grown, ((0, 0), (0, 0), (1, 1), (0, 0)))
    return jnp.concatenate([padded[:, :, k : k + across] for k in range(3)], axis=-1)


def taps(joined, piece):
    count = joined.shape[0] - 2
    tall = joined.shape[1] - 2
    across = joined.shape[2]
    inner = piece.shape[2]
    total = jnp.zeros((count * tall * across, piece.shape[3]), jnp.float32)
    for step_t in range(3):
        for step_r in range(3):
            window = joined[step_t : step_t + count, step_r : step_r + tall].reshape(-1, inner)
            total = total + jnp.dot(
                window, piece[step_t, step_r], preferred_element_type=jnp.float32
            )
    return total.reshape(count, tall, across, piece.shape[3])


def local(latent, gain_first, weight_first, bias_first, gain_second, weight_second, bias_second):
    frames, rows, width, chans = latent.shape
    depth = 1
    first = activate(latent, gain_first).astype(jnp.bfloat16)
    earlier = shifted(first[frames - 2 :], "group", 1)
    stacked = jnp.concatenate([earlier, first], axis=0)
    grown = with_halo(stacked, (("tile", 1),), depth)
    joined_first = widen(grown)
    hidden = (
        taps(joined_first, lax.all_gather(weight_first, "group", axis=2, tiled=True)) + bias_first
    )
    second = activate(hidden, gain_second)
    second = second.astype(jnp.bfloat16)
    later = shifted(second[frames - 2 :], "group", 1)
    second = jnp.concatenate([later, second], axis=0)
    second = with_halo(second, (("tile", 1),), 1)
    joined_second = widen(second)
    branch = taps(joined_second, lax.all_gather(weight_second, "group", axis=2, tiled=True))
    result = latent.astype(jnp.float32) + branch + bias_second
    return result.astype(jnp.bfloat16)


BF16, F32 = jnp.bfloat16, jnp.float32
MESH = pl.DeviceIdType.MESH
UNITS = 18
AHEAD = 3
LAG = 1


def act_slab(wide, gain):
    square = jnp.sum(wide * wide, axis=-1, keepdims=True) * (1.0 / wide.shape[-1])
    scaled = wide * lax.rsqrt(square + 1e-06) * gain
    return scaled / (1.0 + jnp.exp(-scaled))


def fused(
    latent, gain_first_in, weight_first, bias_first_in, gain_second_in, weight_second, bias_second_in, out,
    taps_all, lat, sec, cols, total, gain_first, bias_first, gain_second, bias_second,
    load_sem, lat_sem, line_sem, z_send, z_recv, xy_send, xy_recv, core_send, core_recv, halo_send, halo_recv,
):
    tile, group = lax.axis_index("tile"), lax.axis_index("group")
    tiles, groups = lax.axis_size("tile"), lax.axis_size("group")
    y, x = tile // 2, tile % 2
    z, core = group // 2, group % 2
    zs = groups // 2
    frames, rows, across, chans = latent.shape
    x_tile, y_tile = 2 * y + (1 - x), 2 * (1 - y) + x
    z_part = x + 2 * y - 3 * x * y
    x_part = x + 2 * y - 2 * x * y
    y_part = x + 2 * y - x * y
    corner = (x + y) == 2

    lat[...] = jnp.zeros_like(lat)
    sec[...] = jnp.zeros_like(sec)
    total[...] = jnp.zeros_like(total)


    def load(at):
        source, low, count, start = ((weight_first, 0, 1, 0), (weight_first, 1, 8, 1), (weight_second, 0, 9, 9))[at]
        return pltpu.make_async_copy(
            source.at[pl.ds(low, count)],
            taps_all.at[pl.ds(start, count), z, pl.ds(3 * core, 3)],
            load_sem.at[at],
        )

    line_copies = [
        pltpu.make_async_copy(source, line, line_sem.at[at])
        for at, (source, line) in enumerate(
            (
                (gain_first_in, gain_first),
                (bias_first_in, bias_first),
                (gain_second_in, gain_second),
                (bias_second_in, bias_second),
            )
        )
    ]

    lat_copy = pltpu.make_async_copy(
        latent, lat.at[pl.ds(2, frames), pl.ds(1, rows)], lat_sem
    )
    load(0).start()
    lat_copy.start()
    load(1).start()
    load(2).start()
    for copy in line_copies:
        copy.start()

    barrier = pltpu.get_barrier_semaphore()
    partners = [
        ({"group": group + 2}, z < zs - 1),
        ({"group": group - 2}, z > 0),
        ({"group": group + 1}, group < groups - 1),
        ({"group": group - 1}, group > 0),
        ({"tile": tile + 1}, tile < tiles - 1),
        ({"tile": tile - 1}, tile > 0),
        ({"tile": x_tile}, None),
        ({"tile": y_tile}, None),
    ]
    expected = 0
    for where, there in partners:
        if there is None:
            pl.semaphore_signal(barrier, inc=1, device_id=where, device_id_type=MESH)
            expected = expected + 1
        else:
            @pl.when(there)
            def _():
                pl.semaphore_signal(barrier, inc=1, device_id=where, device_id_type=MESH)
            expected = expected + there.astype(jnp.int32)
    pl.semaphore_wait(barrier, expected)

    def piece(unit, part, origin, where, send, recv):
        block = taps_all.at[unit, origin, 3 * core + part]
        return pltpu.make_async_remote_copy(
            src_ref=block, dst_ref=block, send_sem=send, recv_sem=recv,
            device_id=where, device_id_type=MESH,
        )

    def up(unit, dist):
        return piece(unit, z_part, z - dist, {"group": group + 2}, z_send.at[unit], z_recv.at[unit, 0, dist])

    def down(unit, dist):
        return piece(unit, z_part, z + dist, {"group": group - 2}, z_send.at[unit], z_recv.at[unit, 1, dist])

    def along_x(unit, step):
        return piece(unit, x_part, (z + step) % zs, {"tile": x_tile}, xy_send.at[unit], xy_recv.at[unit, 0])

    def along_y(unit, step):
        return piece(unit, y_part, (z + step) % zs, {"tile": y_tile}, xy_send.at[unit], xy_recv.at[unit, 1])

    def wait_pieces(count, sem):
        block = taps_all.at[0, 0, pl.ds(0, count)]
        pltpu.make_async_copy(block, block, sem).wait()

    def across_cores(unit):
        block = taps_all.at[unit, :, pl.ds(3 * core, 3)]
        return pltpu.make_async_remote_copy(
            src_ref=block, dst_ref=block, send_sem=core_send.at[unit], recv_sem=core_recv.at[unit],
            device_id={"group": 2 * z + (1 - core)}, device_id_type=MESH,
        )

    def own(unit):
        @pl.when(z < zs - 1)
        def _():
            up(unit, 0).start()

        @pl.when(z > 0)
        def _():
            down(unit, 0).start()

    def hand_on(unit, step):
        @pl.when(jnp.logical_not(corner))
        def _():
            along_x(unit, step).start()
            along_y(unit, step).start()

    def arrived(unit, dist):
        @pl.when(z >= dist)
        def _():
            up(unit, dist - 1).wait_recv()
            if dist < zs - 1:
                @pl.when(z < zs - 1)
                def _():
                    up(unit, dist).start()
            hand_on(unit, zs - dist)

        @pl.when(z + dist < zs)
        def _():
            down(unit, dist - 1).wait_recv()
            if dist < zs - 1:
                @pl.when(z > 0)
                def _():
                    down(unit, dist).start()
            hand_on(unit, dist)

    def frame_copy(buf, which):
        return pltpu.make_async_remote_copy(
            src_ref=buf.at[pl.ds(frames, 2), pl.ds(1, rows)], dst_ref=buf.at[pl.ds(0, 2), pl.ds(1, rows)],
            send_sem=halo_send.at[which, 0], recv_sem=halo_recv.at[which, 0],
            device_id={"group": group + 1}, device_id_type=MESH,
        )

    def row_copy(buf, which, later):
        return pltpu.make_async_remote_copy(
            src_ref=buf.at[:, rows if later else 1], dst_ref=buf.at[:, 0 if later else rows + 1],
            send_sem=halo_send.at[which, 1 + later], recv_sem=halo_recv.at[which, 1 + later],
            device_id={"tile": tile + 1 if later else tile - 1}, device_id_type=MESH,
        )

    def send_frames(buf, which):
        @pl.when(group < groups - 1)
        def _():
            frame_copy(buf, which).start()

    def send_rows(buf, which):
        @pl.when(group > 0)
        def _():
            frame_copy(buf, which).wait_recv()

        @pl.when(tile < tiles - 1)
        def _():
            row_copy(buf, which, 1).start()

        @pl.when(tile > 0)
        def _():
            row_copy(buf, which, 0).start()

    def await_rows(buf, which):
        @pl.when(tile > 0)
        def _():
            row_copy(buf, which, 1).wait_recv()

        @pl.when(tile < tiles - 1)
        def _():
            row_copy(buf, which, 0).wait_recv()

    column = lax.broadcasted_iota(jnp.int32, (across, chans), 0)

    def spread(frame, row, value):
        before = jnp.where(column == 0, 0.0, pltpu.roll(value, 1, 0))
        after = jnp.where(column == across - 1, 0.0, pltpu.roll(value, across - 1, 0))
        cols[frame, row, :, 0:chans] = before.astype(BF16)
        cols[frame, row, :, chans : 2 * chans] = value.astype(BF16)
        cols[frame, row, :, 2 * chans : 3 * chans] = after.astype(BF16)

    def first_columns():
        def step(frame, carry):
            for row in range(rows + 2):
                spread(frame, row, act_slab(lat[frame, row].astype(F32), gain_first[...][None]))
            return carry
        lax.fori_loop(0, frames + 2, step, 0)

    def second_values():
        def step(frame, carry):
            for row in range(rows):
                hidden = total[frame, row] + bias_first[...][None]
                sec[frame + 2, row + 1] = act_slab(hidden, gain_second[...][None]).astype(BF16)
            return carry
        lax.fori_loop(0, frames, step, 0)
        total[...] = jnp.zeros_like(total)

    def second_columns():
        def step(frame, carry):
            for row in range(rows + 2):
                spread(frame, row, sec[frame, row].astype(F32))
            return carry
        lax.fori_loop(0, frames + 2, step, 0)

    def multiply(unit):
        step_t, step_r = (unit % 9) // 3, unit % 3
        window = cols[pl.ds(step_t, frames), pl.ds(step_r, rows)].reshape(-1, 3 * chans)
        weight = taps_all[unit].reshape(3 * chans, chans)
        added = jnp.dot(window, weight, preferred_element_type=F32)
        total[...] += added.reshape(frames, rows, across, chans)

    load(0).wait()
    own(0)
    lat_copy.wait()
    load(1).wait()
    for unit in range(1, AHEAD):
        own(unit)
    send_frames(lat, 0)
    load(2).wait()
    for copy in line_copies:
        copy.wait()

    def stage(index, lag, body):
        unit = index - lag

        @pl.when((unit >= 0) & (unit < UNITS))
        def _():
            body(unit)

    def direct(unit):
        @pl.when(tile != 2)
        def _():
            wait_pieces(3, xy_recv.at[unit, 0])

        @pl.when(tile != 1)
        def _():
            wait_pieces(3, xy_recv.at[unit, 1])

        @pl.when(corner)
        def _():
            for step in range(1, zs):
                along_x(unit, step).start()
                along_y(unit, step).start()

    def forwarded(unit):
        @pl.when(tile == 2)
        def _():
            wait_pieces(3, xy_recv.at[unit, 0])

        @pl.when(tile == 1)
        def _():
            wait_pieces(3, xy_recv.at[unit, 1])
        across_cores(unit).start()

    def compute(unit, carry):
        across_cores(unit).wait_recv()
        multiply(unit)
        return carry

    def drain(unit):
        @pl.when((z > 0) & (z < zs - 1))
        def _():
            wait_pieces(zs + 1, z_send.at[unit])

        @pl.when((z == 0) | (z == zs - 1))
        def _():
            wait_pieces(1, z_send.at[unit])
        wait_pieces(2 * zs - 2, xy_send.at[unit])
        across_cores(unit).wait_send()

    half = UNITS // 2
    direct_lag = LAG * (zs - 1)
    forward_lag = direct_lag + LAG
    first_lag = forward_lag + LAG
    middle = half - 1 + first_lag
    drain_lag = first_lag + 4
    turns = UNITS + forward_lag + 1

    def done_by(index):
        first = jnp.clip(index - first_lag + 1, 0, half)
        second = jnp.clip(jnp.minimum(2 * (index - middle - 2), index - forward_lag - half), 0, half)
        return first + second

    def turn(index, carry):
        stage(index, -AHEAD, own)
        for dist in range(1, zs):
            stage(index, LAG * (dist - 1), lambda unit: arrived(unit, dist))
        stage(index, direct_lag, direct)
        stage(index, forward_lag, forwarded)
        stage(index, drain_lag, drain)
        lax.fori_loop(done_by(index - 1), done_by(index), compute, 0)

        @pl.when(index == 1)
        def _():
            send_rows(lat, 0)

        @pl.when(index == 3)
        def _():
            await_rows(lat, 0)
            first_columns()

        @pl.when(index == middle)
        def _():
            second_values()
            send_frames(sec, 1)

        @pl.when(index == middle + 1)
        def _():
            send_rows(sec, 1)

        @pl.when(index == middle + 2)
        def _():
            await_rows(sec, 1)
            second_columns()
        return carry

    lax.fori_loop(0, turns, turn, 0)

    def finish(frame, carry):
        for row in range(rows):
            value = lat[frame + 2, row + 1].astype(F32) + total[frame, row] + bias_second[...][None]
            out[frame, row] = value.astype(BF16)
        return carry
    lax.fori_loop(0, frames, finish, 0)

    def drain_rest(unit, carry):
        drain(unit)
        return carry
    lax.fori_loop(turns - drain_lag, UNITS, drain_rest, 0)
    for which, buf in enumerate((lat, sec)):
        @pl.when(group < groups - 1)
        def _():
            frame_copy(buf, which).wait_send()

        @pl.when(tile < tiles - 1)
        def _():
            row_copy(buf, which, 1).wait_send()

        @pl.when(tile > 0)
        def _():
            row_copy(buf, which, 0).wait_send()


def fused_local(latent, gain_first, weight_first, bias_first, gain_second, weight_second, bias_second):
    frames, rows, across, chans = latent.shape
    depth, zs = weight_first.shape[2], lax.axis_size("group") // 2
    flat = lambda weight: weight.reshape(9, 3, depth // 3, chans)
    anywhere = pl.BlockSpec(memory_space=pl.ANY)
    return pl.pallas_call(
        fused,
        out_shape=jax.ShapeDtypeStruct(latent.shape, BF16),
        in_specs=[anywhere] * 7,
        out_specs=pl.BlockSpec(memory_space=pltpu.VMEM),
        scratch_shapes=[
            pltpu.VMEM((UNITS, zs, 6, depth // 3, chans), BF16),
            pltpu.VMEM((frames + 2, rows + 2, across, chans), BF16),
            pltpu.VMEM((frames + 2, rows + 2, across, chans), BF16),
            pltpu.VMEM((frames + 2, rows + 2, across, 3 * chans), BF16),
            pltpu.VMEM((frames, rows, across, chans), F32),
            *[pltpu.VMEM((chans,), F32)] * 4,
            pltpu.SemaphoreType.DMA((3,)),
            pltpu.SemaphoreType.DMA,
            pltpu.SemaphoreType.DMA((4,)),
            pltpu.SemaphoreType.DMA((UNITS,)),
            pltpu.SemaphoreType.DMA((UNITS, 2, zs - 1)),
            pltpu.SemaphoreType.DMA((UNITS,)),
            pltpu.SemaphoreType.DMA((UNITS, 2)),
            pltpu.SemaphoreType.DMA((UNITS,)),
            pltpu.SemaphoreType.DMA((UNITS,)),
            pltpu.SemaphoreType.DMA((2, 3)),
            pltpu.SemaphoreType.DMA((2, 3)),
        ],
        compiler_params=pltpu.CompilerParams(
            collective_id=0, has_side_effects=True, vmem_limit_bytes=60 * 1024 * 1024
        ),
        cost_estimate=pl.CostEstimate(
            flops=4 * frames * rows * across * 27 * chans * chans,
            bytes_accessed=4 * 9 * depth * chans + 4 * frames * rows * across * chans,
            transcendentals=0,
        ),
    )(latent, gain_first, flat(weight_first), bias_first, gain_second, flat(weight_second), bias_second)


def solution(mesh):
    small = mesh.shape["tile"] == 4 and mesh.shape["group"] == 8
    return jax.shard_map(
        fused_local if small else local,
        mesh=mesh,
        in_specs=(
            P(("cand", "group"), "tile", None, None),
            P(),
            P(None, None, "group", None),
            P(),
            P(),
            P(None, None, "group", None),
            P(),
        ),
        out_specs=P(("cand", "group"), "tile", None, None),
        check_vma=False,
    )
```

```python
import jax
import jax.numpy as jnp
from jax import lax
from jax.experimental import pallas as pl
from jax.experimental.pallas import tpu as pltpu
from jax.sharding import PartitionSpec as P


def shifted(value, axis, steps):
    count = lax.axis_size(axis)
    first, last = (max(0, -steps), min(count, count - steps))
    return lax.ppermute(value, axis, [(source, source + steps) for source in range(first, last)])


def with_halo(array, sides, width):
    for axis, dim in sides:
        size, length = (lax.axis_size(axis), array.shape[dim])
        up = [(i, (i + 1) % size) for i in range(size - 1)]
        down = [(j, i) for i, j in up]
        last = lax.slice_in_dim(array, length - width, length, axis=dim)
        first = lax.slice_in_dim(array, 0, width, axis=dim)
        before = lax.ppermute(last, axis, up)
        after = lax.ppermute(first, axis, down)
        array = jnp.concatenate([before, array, after], axis=dim)
    return array


def activate(values, gain):
    wide = values.astype(jnp.float32)
    scaled = wide * lax.rsqrt(jnp.mean(wide * wide, axis=-1, keepdims=True) + 1e-06) * gain
    return jax.nn.silu(scaled)


def widen(grown):
    across = grown.shape[2]
    padded = jnp.pad(grown, ((0, 0), (0, 0), (1, 1), (0, 0)))
    return jnp.concatenate([padded[:, :, k : k + across] for k in range(3)], axis=-1)


def taps(joined, piece):
    count = joined.shape[0] - 2
    tall = joined.shape[1] - 2
    across = joined.shape[2]
    inner = piece.shape[2]
    total = jnp.zeros((count * tall * across, piece.shape[3]), jnp.float32)
    for step_t in range(3):
        for step_r in range(3):
            window = joined[step_t : step_t + count, step_r : step_r + tall].reshape(-1, inner)
            total = total + jnp.dot(
                window, piece[step_t, step_r], preferred_element_type=jnp.float32
            )
    return total.reshape(count, tall, across, piece.shape[3])


def local(latent, gain_first, weight_first, bias_first, gain_second, weight_second, bias_second):
    frames, rows, width, chans = latent.shape
    depth = 1
    first = activate(latent, gain_first).astype(jnp.bfloat16)
    earlier = shifted(first[frames - 2 :], "group", 1)
    stacked = jnp.concatenate([earlier, first], axis=0)
    grown = with_halo(stacked, (("tile", 1),), depth)
    joined_first = widen(grown)
    hidden = (
        taps(joined_first, lax.all_gather(weight_first, "group", axis=2, tiled=True)) + bias_first
    )
    second = activate(hidden, gain_second)
    second = second.astype(jnp.bfloat16)
    later = shifted(second[frames - 2 :], "group", 1)
    second = jnp.concatenate([later, second], axis=0)
    second = with_halo(second, (("tile", 1),), 1)
    joined_second = widen(second)
    branch = taps(joined_second, lax.all_gather(weight_second, "group", axis=2, tiled=True))
    result = latent.astype(jnp.float32) + branch + bias_second
    return result.astype(jnp.bfloat16)


BF16, F32 = jnp.bfloat16, jnp.float32
MESH = pl.DeviceIdType.MESH
UNITS = 18
AHEAD = 3
LAG = 2


def act_slab(wide, gain):
    square = jnp.sum(wide * wide, axis=-1, keepdims=True) * (1.0 / wide.shape[-1])
    scaled = wide * lax.rsqrt(square + 1e-06) * gain
    return scaled / (1.0 + jnp.exp(-scaled))


def fused(
    latent, gain_first_in, weight_first, bias_first_in, gain_second_in, weight_second, bias_second_in, out,
    taps_all, lat, sec, cols, total, gain_first, bias_first, gain_second, bias_second,
    load_sem, lat_sem, line_sem, z_send, z_recv, xy_send, xy_recv, core_send, core_recv, halo_send, halo_recv,
):
    tile, group = lax.axis_index("tile"), lax.axis_index("group")
    tiles, groups = lax.axis_size("tile"), lax.axis_size("group")
    y, x = tile // 2, tile % 2
    z, core = group // 2, group % 2
    zs = groups // 2
    frames, rows, across, chans = latent.shape
    x_tile, y_tile = 2 * y + (1 - x), 2 * (1 - y) + x
    z_part = x + 2 * y - 3 * x * y
    x_part = x + 2 * y - 2 * x * y
    y_part = x + 2 * y - x * y
    corner = (x + y) == 2

    lat[...] = jnp.zeros_like(lat)
    sec[...] = jnp.zeros_like(sec)
    total[...] = jnp.zeros_like(total)


    def load(at):
        source, low, count, start = ((weight_first, 0, 1, 0), (weight_first, 1, 8, 1), (weight_second, 0, 9, 9))[at]
        return pltpu.make_async_copy(
            source.at[pl.ds(low, count)],
            taps_all.at[pl.ds(start, count), z, pl.ds(3 * core, 3)],
            load_sem.at[at],
        )

    line_copies = [
        pltpu.make_async_copy(source, line, line_sem.at[at])
        for at, (source, line) in enumerate(
            (
                (gain_first_in, gain_first),
                (bias_first_in, bias_first),
                (gain_second_in, gain_second),
                (bias_second_in, bias_second),
            )
        )
    ]

    lat_copy = pltpu.make_async_copy(
        latent, lat.at[pl.ds(2, frames), pl.ds(1, rows)], lat_sem
    )
    load(0).start()
    lat_copy.start()
    load(1).start()
    load(2).start()
    for copy in line_copies:
        copy.start()

    barrier = pltpu.get_barrier_semaphore()
    partners = [
        ({"group": group + 2}, z < zs - 1),
        ({"group": group - 2}, z > 0),
        ({"group": group + 4}, z < zs - 2),
        ({"group": group - 4}, z > 1),
        ({"tile": tile + 1, "group": group + 1}, (tile < tiles - 1) & (group < groups - 1)),
        ({"tile": tile - 1, "group": group + 1}, (tile > 0) & (group < groups - 1)),
        ({"tile": tile + 1, "group": group - 1}, (tile < tiles - 1) & (group > 0)),
        ({"tile": tile - 1, "group": group - 1}, (tile > 0) & (group > 0)),
        ({"group": group + 1}, group < groups - 1),
        ({"group": group - 1}, group > 0),
        ({"tile": tile + 1}, tile < tiles - 1),
        ({"tile": tile - 1}, tile > 0),
        ({"tile": x_tile}, None),
        ({"tile": y_tile}, None),
    ]
    expected = 0
    for where, there in partners:
        if there is None:
            pl.semaphore_signal(barrier, inc=1, device_id=where, device_id_type=MESH)
            expected = expected + 1
        else:
            @pl.when(there)
            def _():
                pl.semaphore_signal(barrier, inc=1, device_id=where, device_id_type=MESH)
            expected = expected + there.astype(jnp.int32)
    pl.semaphore_wait(barrier, expected)

    def piece(unit, part, origin, where, send, recv):
        block = taps_all.at[unit, origin, 3 * core + part]
        return pltpu.make_async_remote_copy(
            src_ref=block, dst_ref=block, send_sem=send, recv_sem=recv,
            device_id=where, device_id_type=MESH,
        )

    def along_z(unit, origin, delta):
        slot = (origin - (z + delta) + zs) % zs - 1
        return piece(unit, z_part, origin, {"group": group + 2 * delta}, z_send.at[unit], z_recv.at[unit, slot])

    def along_x(unit, origin):
        return piece(unit, x_part, origin, {"tile": x_tile}, xy_send.at[unit], xy_recv.at[unit, 0])

    def along_y(unit, origin):
        return piece(unit, y_part, origin, {"tile": y_tile}, xy_send.at[unit], xy_recv.at[unit, 1])

    def wait_pieces(count, sem):
        block = taps_all.at[0, 0, pl.ds(0, count)]
        pltpu.make_async_copy(block, block, sem).wait()

    def across_cores(unit):
        block = taps_all.at[unit, :, pl.ds(3 * core, 3)]
        return pltpu.make_async_remote_copy(
            src_ref=block, dst_ref=block, send_sem=core_send.at[unit], recv_sem=core_recv.at[unit],
            device_id={"group": 2 * z + (1 - core)}, device_id_type=MESH,
        )

    at_end = (z == 0) | (z == zs - 1)
    low_side = (z < 2).astype(jnp.int32)
    inward = 2 * low_side - 1

    def own(unit):
        along_z(unit, z, inward).start()

        @pl.when(at_end)
        def _():
            along_z(unit, z, 2 * inward).start()

        @pl.when(jnp.logical_not(at_end))
        def _():
            along_z(unit, z, -inward).start()

    def hand_on(unit, origin):
        @pl.when(jnp.logical_not(corner))
        def _():
            along_x(unit, origin).start()
            along_y(unit, origin).start()

    def await_z(unit, origin):
        wait_pieces(1, z_recv.at[unit, (origin - z + zs) % zs - 1])

    def near(unit):
        @pl.when(at_end)
        def _():
            await_z(unit, z + inward)
            hand_on(unit, z + inward)

        @pl.when(jnp.logical_not(at_end))
        def _():
            await_z(unit, z + inward)
            along_z(unit, z + inward, -inward).start()
            hand_on(unit, z + inward)
            await_z(unit, z - inward)
            hand_on(unit, z - inward)
            await_z(unit, z + 2 * inward)
            along_z(unit, z + 2 * inward, -inward).start()
            hand_on(unit, z + 2 * inward)

    def far(unit):
        @pl.when(at_end)
        def _():
            for steps in (2, 3):
                await_z(unit, z + steps * inward)
                hand_on(unit, z + steps * inward)

    def halo_copies(buf, which):
        late, low, high = pl.ds(frames, 2), tile > 0, tile < tiles - 1
        sends, gets = group < groups - 1, group > 0
        inner, body = pl.ds(1, rows), pl.ds(2, frames)
        plan = (
            ((late, inner), (pl.ds(0, 2), inner), {"group": group + 1}, sends, gets),
            ((body, rows), (body, 0), {"tile": tile + 1}, high, low),
            ((body, 1), (body, rows + 1), {"tile": tile - 1}, low, high),
            ((late, rows), (pl.ds(0, 2), 0), {"tile": tile + 1, "group": group + 1}, sends & high, gets & low),
            ((late, 1), (pl.ds(0, 2), rows + 1), {"tile": tile - 1, "group": group + 1}, sends & low, gets & high),
        )
        for at, (source, target, where, there, here) in enumerate(plan):
            copy = pltpu.make_async_remote_copy(
                src_ref=buf.at[source], dst_ref=buf.at[target],
                send_sem=halo_send.at[which, at], recv_sem=halo_recv.at[which, at],
                device_id=where, device_id_type=MESH,
            )
            yield copy, there, here

    def send_halo(buf, which):
        for copy, there, _ in halo_copies(buf, which):
            pl.when(there)(copy.start)

    def await_halo(buf, which):
        for copy, _, here in halo_copies(buf, which):
            pl.when(here)(copy.wait_recv)

    column = lax.broadcasted_iota(jnp.int32, (across, chans), 0)

    def spread(frame, row, value):
        before = jnp.where(column == 0, 0.0, pltpu.roll(value, 1, 0))
        after = jnp.where(column == across - 1, 0.0, pltpu.roll(value, across - 1, 0))
        cols[frame, row, :, 0:chans] = before.astype(BF16)
        cols[frame, row, :, chans : 2 * chans] = value.astype(BF16)
        cols[frame, row, :, 2 * chans : 3 * chans] = after.astype(BF16)

    def first_columns():
        def step(frame, carry):
            for row in range(rows + 2):
                spread(frame, row, act_slab(lat[frame, row].astype(F32), gain_first[...][None]))
            return carry
        lax.fori_loop(0, frames + 2, step, 0)

    def second_values():
        def step(frame, carry):
            for row in range(rows):
                hidden = total[frame, row] + bias_first[...][None]
                sec[frame + 2, row + 1] = act_slab(hidden, gain_second[...][None]).astype(BF16)
            return carry
        lax.fori_loop(0, frames, step, 0)
        total[...] = jnp.zeros_like(total)

    def second_columns():
        def step(frame, carry):
            for row in range(rows + 2):
                spread(frame, row, sec[frame, row].astype(F32))
            return carry
        lax.fori_loop(0, frames + 2, step, 0)

    def multiply(unit):
        step_t, step_r = (unit % 9) // 3, unit % 3
        window = cols[pl.ds(step_t, frames), pl.ds(step_r, rows)].reshape(-1, 3 * chans)
        weight = taps_all[unit].reshape(3 * chans, chans)
        added = jnp.dot(window, weight, preferred_element_type=F32)
        total[...] += added.reshape(frames, rows, across, chans)

    load(0).wait()
    own(0)
    lat_copy.wait()
    load(1).wait()
    for unit in range(1, AHEAD):
        own(unit)
    send_halo(lat, 0)
    load(2).wait()
    for copy in line_copies:
        copy.wait()

    def stage(index, lag, body):
        unit = index - lag

        @pl.when((unit >= 0) & (unit < UNITS))
        def _():
            body(unit)

    def direct(unit):
        @pl.when(tile != 2)
        def _():
            wait_pieces(3, xy_recv.at[unit, 0])

        @pl.when(tile != 1)
        def _():
            wait_pieces(3, xy_recv.at[unit, 1])

        @pl.when(corner)
        def _():
            for step in range(1, zs):
                along_x(unit, (z + step) % zs).start()
                along_y(unit, (z + step) % zs).start()

    def forwarded(unit):
        @pl.when(tile == 2)
        def _():
            wait_pieces(3, xy_recv.at[unit, 0])

        @pl.when(tile == 1)
        def _():
            wait_pieces(3, xy_recv.at[unit, 1])
        across_cores(unit).start()

    def compute(unit, carry):
        across_cores(unit).wait_recv()
        multiply(unit)
        return carry

    def drain(unit):
        @pl.when(at_end)
        def _():
            wait_pieces(2, z_send.at[unit])

        @pl.when(jnp.logical_not(at_end))
        def _():
            wait_pieces(4, z_send.at[unit])
        wait_pieces(2 * zs - 2, xy_send.at[unit])
        across_cores(unit).wait_send()

    half = UNITS // 2
    direct_lag = 2 * LAG
    forward_lag = direct_lag + LAG
    first_lag = forward_lag + 1
    middle = half - 1 + first_lag
    drain_lag = first_lag + 4
    turns = UNITS + first_lag

    def done_by(index):
        first = jnp.clip(index - first_lag + 1, 0, half)
        second = jnp.clip(jnp.minimum(2 * (index - middle - 1), index - first_lag - half + 1), 0, half)
        return first + second

    def turn(index, carry):
        stage(index, -AHEAD, own)
        stage(index, 0, near)
        stage(index, LAG, far)
        stage(index, direct_lag, direct)
        stage(index, forward_lag, forwarded)
        stage(index, drain_lag, drain)
        lax.fori_loop(done_by(index - 1), done_by(index), compute, 0)

        @pl.when(index == 2)
        def _():
            await_halo(lat, 0)
            first_columns()

        @pl.when(index == middle)
        def _():
            second_values()
            send_halo(sec, 1)

        @pl.when(index == middle + 1)
        def _():
            await_halo(sec, 1)
            second_columns()
        return carry

    lax.fori_loop(0, turns, turn, 0)

    def finish(frame, carry):
        for row in range(rows):
            value = lat[frame + 2, row + 1].astype(F32) + total[frame, row] + bias_second[...][None]
            out[frame, row] = value.astype(BF16)
        return carry
    lax.fori_loop(0, frames, finish, 0)

    def drain_rest(unit, carry):
        drain(unit)
        return carry
    lax.fori_loop(turns - drain_lag, UNITS, drain_rest, 0)
    for which, buf in enumerate((lat, sec)):
        for copy, there, _ in halo_copies(buf, which):
            pl.when(there)(copy.wait_send)


def fused_local(latent, gain_first, weight_first, bias_first, gain_second, weight_second, bias_second):
    frames, rows, across, chans = latent.shape
    depth, zs = weight_first.shape[2], lax.axis_size("group") // 2
    flat = lambda weight: weight.reshape(9, 3, depth // 3, chans)
    anywhere = pl.BlockSpec(memory_space=pl.ANY)
    return pl.pallas_call(
        fused,
        out_shape=jax.ShapeDtypeStruct(latent.shape, BF16),
        in_specs=[anywhere] * 7,
        out_specs=pl.BlockSpec(memory_space=pltpu.VMEM),
        scratch_shapes=[
            pltpu.VMEM((UNITS, zs, 6, depth // 3, chans), BF16),
            pltpu.VMEM((frames + 2, rows + 2, across, chans), BF16),
            pltpu.VMEM((frames + 2, rows + 2, across, chans), BF16),
            pltpu.VMEM((frames + 2, rows + 2, across, 3 * chans), BF16),
            pltpu.VMEM((frames, rows, across, chans), F32),
            *[pltpu.VMEM((chans,), F32)] * 4,
            pltpu.SemaphoreType.DMA((3,)),
            pltpu.SemaphoreType.DMA,
            pltpu.SemaphoreType.DMA((4,)),
            pltpu.SemaphoreType.DMA((UNITS,)),
            pltpu.SemaphoreType.DMA((UNITS, zs - 1)),
            pltpu.SemaphoreType.DMA((UNITS,)),
            pltpu.SemaphoreType.DMA((UNITS, 2)),
            pltpu.SemaphoreType.DMA((UNITS,)),
            pltpu.SemaphoreType.DMA((UNITS,)),
            pltpu.SemaphoreType.DMA((2, 5)),
            pltpu.SemaphoreType.DMA((2, 5)),
        ],
        compiler_params=pltpu.CompilerParams(
            collective_id=0, has_side_effects=True, vmem_limit_bytes=60 * 1024 * 1024
        ),
        cost_estimate=pl.CostEstimate(
            flops=4 * frames * rows * across * 27 * chans * chans,
            bytes_accessed=4 * 9 * depth * chans + 4 * frames * rows * across * chans,
            transcendentals=0,
        ),
    )(latent, gain_first, flat(weight_first), bias_first, gain_second, flat(weight_second), bias_second)


def solution(mesh):
    small = mesh.shape["tile"] == 4 and mesh.shape["group"] == 8
    return jax.shard_map(
        fused_local if small else local,
        mesh=mesh,
        in_specs=(
            P(("cand", "group"), "tile", None, None),
            P(),
            P(None, None, "group", None),
            P(),
            P(),
            P(None, None, "group", None),
            P(),
        ),
        out_specs=P(("cand", "group"), "tile", None, None),
        check_vma=False,
    )
```

```python
import jax
import jax.numpy as jnp
from jax import lax
from jax.experimental import pallas as pl
from jax.experimental.pallas import tpu as pltpu
from jax.sharding import PartitionSpec as P


def shifted(value, axis, steps):
    count = lax.axis_size(axis)
    first, last = (max(0, -steps), min(count, count - steps))
    return lax.ppermute(value, axis, [(source, source + steps) for source in range(first, last)])


def with_halo(array, sides, width):
    for axis, dim in sides:
        size, length = (lax.axis_size(axis), array.shape[dim])
        up = [(i, (i + 1) % size) for i in range(size - 1)]
        down = [(j, i) for i, j in up]
        last = lax.slice_in_dim(array, length - width, length, axis=dim)
        first = lax.slice_in_dim(array, 0, width, axis=dim)
        before = lax.ppermute(last, axis, up)
        after = lax.ppermute(first, axis, down)
        array = jnp.concatenate([before, array, after], axis=dim)
    return array


def activate(values, gain):
    wide = values.astype(jnp.float32)
    scaled = wide * lax.rsqrt(jnp.mean(wide * wide, axis=-1, keepdims=True) + 1e-06) * gain
    return jax.nn.silu(scaled)


def widen(grown):
    across = grown.shape[2]
    padded = jnp.pad(grown, ((0, 0), (0, 0), (1, 1), (0, 0)))
    return jnp.concatenate([padded[:, :, k : k + across] for k in range(3)], axis=-1)


def taps(joined, piece):
    count = joined.shape[0] - 2
    tall = joined.shape[1] - 2
    across = joined.shape[2]
    inner = piece.shape[2]
    total = jnp.zeros((count * tall * across, piece.shape[3]), jnp.float32)
    for step_t in range(3):
        for step_r in range(3):
            window = joined[step_t : step_t + count, step_r : step_r + tall].reshape(-1, inner)
            total = total + jnp.dot(
                window, piece[step_t, step_r], preferred_element_type=jnp.float32
            )
    return total.reshape(count, tall, across, piece.shape[3])


def local(latent, gain_first, weight_first, bias_first, gain_second, weight_second, bias_second):
    frames, rows, width, chans = latent.shape
    depth = 1
    first = activate(latent, gain_first).astype(jnp.bfloat16)
    earlier = shifted(first[frames - 2 :], "group", 1)
    stacked = jnp.concatenate([earlier, first], axis=0)
    grown = with_halo(stacked, (("tile", 1),), depth)
    joined_first = widen(grown)
    hidden = (
        taps(joined_first, lax.all_gather(weight_first, "group", axis=2, tiled=True)) + bias_first
    )
    second = activate(hidden, gain_second)
    second = second.astype(jnp.bfloat16)
    later = shifted(second[frames - 2 :], "group", 1)
    second = jnp.concatenate([later, second], axis=0)
    second = with_halo(second, (("tile", 1),), 1)
    joined_second = widen(second)
    branch = taps(joined_second, lax.all_gather(weight_second, "group", axis=2, tiled=True))
    result = latent.astype(jnp.float32) + branch + bias_second
    return result.astype(jnp.bfloat16)


BF16, F32 = jnp.bfloat16, jnp.float32
MESH = pl.DeviceIdType.MESH
UNITS = 18
AHEAD = 3
LAG = 2


def act_slab(wide, gain):
    square = jnp.sum(wide * wide, axis=-1, keepdims=True) * (1.0 / wide.shape[-1])
    scaled = wide * lax.rsqrt(square + 1e-06) * gain
    return scaled / (1.0 + jnp.exp(-scaled))


def fused(
    latent, gain_first_in, weight_first, bias_first_in, gain_second_in, weight_second, bias_second_in, out,
    taps_all, lat, sec, cols, total, gain_first, bias_first, gain_second, bias_second,
    load_sem, lat_sem, line_sem, z_send, z_recv, xy_send, xy_recv, core_send, core_recv, halo_send, halo_recv,
):
    tile, group = lax.axis_index("tile"), lax.axis_index("group")
    tiles, groups = lax.axis_size("tile"), lax.axis_size("group")
    y, x = tile // 2, tile % 2
    z, core = group // 2, group % 2
    zs = groups // 2
    frames, rows, across, chans = latent.shape
    x_tile, y_tile = 2 * y + (1 - x), 2 * (1 - y) + x
    z_part = x + 2 * y - 3 * x * y
    x_part = x + 2 * y - 2 * x * y
    y_part = x + 2 * y - x * y
    corner = (x + y) == 2

    lat[...] = jnp.zeros_like(lat)
    sec[...] = jnp.zeros_like(sec)


    def load(at):
        source, low, count, start = ((weight_first, 0, 1, 0), (weight_first, 1, 8, 1), (weight_second, 0, 9, 9))[at]
        return pltpu.make_async_copy(
            source.at[pl.ds(low, count)],
            taps_all.at[pl.ds(start, count), z, pl.ds(3 * core, 3)],
            load_sem.at[at],
        )

    line_copies = [
        pltpu.make_async_copy(source, line, line_sem.at[at])
        for at, (source, line) in enumerate(
            (
                (gain_first_in, gain_first),
                (bias_first_in, bias_first),
                (gain_second_in, gain_second),
                (bias_second_in, bias_second),
            )
        )
    ]

    lat_copy = pltpu.make_async_copy(
        latent, lat.at[pl.ds(2, frames), pl.ds(1, rows)], lat_sem
    )
    load(0).start()
    lat_copy.start()
    load(1).start()
    load(2).start()
    for copy in line_copies:
        copy.start()

    barrier = pltpu.get_barrier_semaphore()
    partners = [
        ({"group": group + 2}, z < zs - 1),
        ({"group": group - 2}, z > 0),
        ({"group": group + 4}, z < zs - 2),
        ({"group": group - 4}, z > 1),
        ({"tile": tile + 1, "group": group + 1}, (tile < tiles - 1) & (group < groups - 1)),
        ({"tile": tile - 1, "group": group + 1}, (tile > 0) & (group < groups - 1)),
        ({"tile": tile + 1, "group": group - 1}, (tile < tiles - 1) & (group > 0)),
        ({"tile": tile - 1, "group": group - 1}, (tile > 0) & (group > 0)),
        ({"group": group + 1}, group < groups - 1),
        ({"group": group - 1}, group > 0),
        ({"tile": tile + 1}, tile < tiles - 1),
        ({"tile": tile - 1}, tile > 0),
        ({"tile": x_tile}, None),
        ({"tile": y_tile}, None),
    ]
    expected = 0
    for where, there in partners:
        if there is None:
            pl.semaphore_signal(barrier, inc=1, device_id=where, device_id_type=MESH)
            expected = expected + 1
        else:
            @pl.when(there)
            def _():
                pl.semaphore_signal(barrier, inc=1, device_id=where, device_id_type=MESH)
            expected = expected + there.astype(jnp.int32)
    pl.semaphore_wait(barrier, expected)

    def piece(unit, part, origin, where, send, recv):
        block = taps_all.at[unit, origin, 3 * core + part]
        return pltpu.make_async_remote_copy(
            src_ref=block, dst_ref=block, send_sem=send, recv_sem=recv,
            device_id=where, device_id_type=MESH,
        )

    def along_z(unit, origin, delta):
        slot = (origin - (z + delta) + zs) % zs - 1
        return piece(unit, z_part, origin, {"group": group + 2 * delta}, z_send.at[unit], z_recv.at[unit, slot])

    def along_x(unit, origin):
        return piece(unit, x_part, origin, {"tile": x_tile}, xy_send.at[unit], xy_recv.at[unit, 0])

    def along_y(unit, origin):
        return piece(unit, y_part, origin, {"tile": y_tile}, xy_send.at[unit], xy_recv.at[unit, 1])

    def wait_pieces(count, sem):
        block = taps_all.at[0, 0, pl.ds(0, count)]
        pltpu.make_async_copy(block, block, sem).wait()

    def across_cores(unit):
        block = taps_all.at[unit, :, pl.ds(3 * core, 3)]
        return pltpu.make_async_remote_copy(
            src_ref=block, dst_ref=block, send_sem=core_send.at[unit], recv_sem=core_recv.at[unit],
            device_id={"group": 2 * z + (1 - core)}, device_id_type=MESH,
        )

    at_end = (z == 0) | (z == zs - 1)
    low_side = (z < 2).astype(jnp.int32)
    inward = 2 * low_side - 1

    def own(unit):
        along_z(unit, z, inward).start()

        @pl.when(at_end)
        def _():
            along_z(unit, z, 2 * inward).start()

        @pl.when(jnp.logical_not(at_end))
        def _():
            along_z(unit, z, -inward).start()

    def hand_on(unit, origin):
        @pl.when(jnp.logical_not(corner))
        def _():
            along_x(unit, origin).start()
            along_y(unit, origin).start()

    def await_z(unit, origin):
        wait_pieces(1, z_recv.at[unit, (origin - z + zs) % zs - 1])

    def near(unit):
        @pl.when(at_end)
        def _():
            await_z(unit, z + inward)
            hand_on(unit, z + inward)

        @pl.when(jnp.logical_not(at_end))
        def _():
            await_z(unit, z + inward)
            along_z(unit, z + inward, -inward).start()
            hand_on(unit, z + inward)
            await_z(unit, z - inward)
            hand_on(unit, z - inward)
            await_z(unit, z + 2 * inward)
            along_z(unit, z + 2 * inward, -inward).start()
            hand_on(unit, z + 2 * inward)

    def far(unit):
        @pl.when(at_end)
        def _():
            for steps in (2, 3):
                await_z(unit, z + steps * inward)
                hand_on(unit, z + steps * inward)

    def halo_copies(buf, which):
        late, low, high = pl.ds(frames, 2), tile > 0, tile < tiles - 1
        sends, gets = group < groups - 1, group > 0
        inner, body = pl.ds(1, rows), pl.ds(2, frames)
        plan = (
            ((late, inner), (pl.ds(0, 2), inner), {"group": group + 1}, sends, gets),
            ((body, rows), (body, 0), {"tile": tile + 1}, high, low),
            ((body, 1), (body, rows + 1), {"tile": tile - 1}, low, high),
            ((late, rows), (pl.ds(0, 2), 0), {"tile": tile + 1, "group": group + 1}, sends & high, gets & low),
            ((late, 1), (pl.ds(0, 2), rows + 1), {"tile": tile - 1, "group": group + 1}, sends & low, gets & high),
        )
        for at, (source, target, where, there, here) in enumerate(plan):
            copy = pltpu.make_async_remote_copy(
                src_ref=buf.at[source], dst_ref=buf.at[target],
                send_sem=halo_send.at[which, at], recv_sem=halo_recv.at[which, at],
                device_id=where, device_id_type=MESH,
            )
            yield copy, there, here

    def send_halo(buf, which):
        for copy, there, _ in halo_copies(buf, which):
            pl.when(there)(copy.start)

    def await_halo(buf, which):
        for copy, _, here in halo_copies(buf, which):
            pl.when(here)(copy.wait_recv)

    column = lax.broadcasted_iota(jnp.int32, (across, chans), 0)

    def spread(frame, row, value):
        before = jnp.where(column == 0, 0.0, pltpu.roll(value, 1, 0))
        after = jnp.where(column == across - 1, 0.0, pltpu.roll(value, across - 1, 0))
        cols[frame, row, :, 0:chans] = before.astype(BF16)
        cols[frame, row, :, chans : 2 * chans] = value.astype(BF16)
        cols[frame, row, :, 2 * chans : 3 * chans] = after.astype(BF16)

    def first_columns(frame):
        for row in range(rows + 2):
            spread(frame, row, act_slab(lat[frame, row].astype(F32), gain_first[...][None]))

    def second_values():
        def step(frame, carry):
            for row in range(rows):
                hidden = total[frame, row] + bias_first[...][None]
                sec[frame + 2, row + 1] = act_slab(hidden, gain_second[...][None]).astype(BF16)
            return carry
        lax.fori_loop(0, frames, step, 0)
        total[...] = jnp.zeros_like(total)

    def second_columns(low, high, chosen):
        def step(frame, carry):
            for row in chosen:
                spread(frame, row, sec[frame, row].astype(F32))
            return carry
        lax.fori_loop(low, high, step, 0)

    def multiply(unit):
        step_t, step_r = (unit % 9) // 3, unit % 3
        window = cols[pl.ds(step_t, frames), pl.ds(step_r, rows)].reshape(-1, 3 * chans)
        weight = taps_all[unit].reshape(3 * chans, chans)
        added = jnp.dot(window, weight, preferred_element_type=F32)
        total[...] += added.reshape(frames, rows, across, chans)

    load(0).wait()
    own(0)
    lat_copy.wait()
    load(1).wait()
    for unit in range(1, AHEAD):
        own(unit)
    send_halo(lat, 0)
    total[...] = jnp.zeros_like(total)
    load(2).wait()
    for copy in line_copies:
        copy.wait()

    def stage(index, lag, body):
        unit = index - lag

        @pl.when((unit >= 0) & (unit < UNITS))
        def _():
            body(unit)

    def direct(unit):
        @pl.when(tile != 2)
        def _():
            wait_pieces(3, xy_recv.at[unit, 0])

        @pl.when(tile != 1)
        def _():
            wait_pieces(3, xy_recv.at[unit, 1])

        @pl.when(corner)
        def _():
            for step in range(1, zs):
                along_x(unit, (z + step) % zs).start()
                along_y(unit, (z + step) % zs).start()

    def forwarded(unit):
        @pl.when(tile == 2)
        def _():
            wait_pieces(3, xy_recv.at[unit, 0])

        @pl.when(tile == 1)
        def _():
            wait_pieces(3, xy_recv.at[unit, 1])
        across_cores(unit).start()

    def compute(unit, carry):
        across_cores(unit).wait_recv()
        multiply(unit)
        return carry

    def drain(unit):
        @pl.when(at_end)
        def _():
            wait_pieces(2, z_send.at[unit])

        @pl.when(jnp.logical_not(at_end))
        def _():
            wait_pieces(4, z_send.at[unit])
        wait_pieces(2 * zs - 2, xy_send.at[unit])
        across_cores(unit).wait_send()

    half = UNITS // 2
    direct_lag = 2 * LAG
    forward_lag = direct_lag + LAG
    first_lag = forward_lag + 1
    assert frames + 2 < first_lag
    middle = half - 1 + first_lag
    drain_lag = first_lag + 4
    turns = UNITS + first_lag

    def done_by(index):
        first = jnp.clip(index - first_lag + 1, 0, half)
        second = jnp.clip(jnp.minimum(2 * (index - middle - 2), index - first_lag - half + 1), 0, half)
        return first + second

    def turn(index, carry):
        stage(index, -AHEAD, own)
        stage(index, 0, near)
        stage(index, LAG, far)
        stage(index, direct_lag, direct)
        stage(index, forward_lag, forwarded)
        stage(index, drain_lag, drain)
        lax.fori_loop(done_by(index - 1), done_by(index), compute, 0)

        @pl.when(index == 1)
        def _():
            await_halo(lat, 0)

        @pl.when((index >= 1) & (index < frames + 3))
        def _():
            first_columns(index - 1)

        @pl.when(index == middle)
        def _():
            second_values()
            send_halo(sec, 1)

        @pl.when(index == middle + 1)
        def _():
            second_columns(2, frames + 2, range(1, rows + 1))

        @pl.when(index == middle + 2)
        def _():
            await_halo(sec, 1)
            second_columns(0, 2, range(rows + 2))
            second_columns(2, frames + 2, (0, rows + 1))
        return carry

    lax.fori_loop(0, turns, turn, 0)

    def finish(frame, carry):
        for row in range(rows):
            value = lat[frame + 2, row + 1].astype(F32) + total[frame, row] + bias_second[...][None]
            out[frame, row] = value.astype(BF16)
        return carry
    lax.fori_loop(0, frames, finish, 0)

    def drain_rest(unit, carry):
        drain(unit)
        return carry
    lax.fori_loop(turns - drain_lag, UNITS, drain_rest, 0)
    for which, buf in enumerate((lat, sec)):
        for copy, there, _ in halo_copies(buf, which):
            pl.when(there)(copy.wait_send)


def fused_local(latent, gain_first, weight_first, bias_first, gain_second, weight_second, bias_second):
    frames, rows, across, chans = latent.shape
    depth, zs = weight_first.shape[2], lax.axis_size("group") // 2
    flat = lambda weight: weight.reshape(9, 3, depth // 3, chans)
    anywhere = pl.BlockSpec(memory_space=pl.ANY)
    return pl.pallas_call(
        fused,
        out_shape=jax.ShapeDtypeStruct(latent.shape, BF16),
        in_specs=[anywhere] * 7,
        out_specs=pl.BlockSpec(memory_space=pltpu.VMEM),
        scratch_shapes=[
            pltpu.VMEM((UNITS, zs, 6, depth // 3, chans), BF16),
            pltpu.VMEM((frames + 2, rows + 2, across, chans), BF16),
            pltpu.VMEM((frames + 2, rows + 2, across, chans), BF16),
            pltpu.VMEM((frames + 2, rows + 2, across, 3 * chans), BF16),
            pltpu.VMEM((frames, rows, across, chans), F32),
            *[pltpu.VMEM((chans,), F32)] * 4,
            pltpu.SemaphoreType.DMA((3,)),
            pltpu.SemaphoreType.DMA,
            pltpu.SemaphoreType.DMA((4,)),
            pltpu.SemaphoreType.DMA((UNITS,)),
            pltpu.SemaphoreType.DMA((UNITS, zs - 1)),
            pltpu.SemaphoreType.DMA((UNITS,)),
            pltpu.SemaphoreType.DMA((UNITS, 2)),
            pltpu.SemaphoreType.DMA((UNITS,)),
            pltpu.SemaphoreType.DMA((UNITS,)),
            pltpu.SemaphoreType.DMA((2, 5)),
            pltpu.SemaphoreType.DMA((2, 5)),
        ],
        compiler_params=pltpu.CompilerParams(
            collective_id=0, has_side_effects=True, vmem_limit_bytes=60 * 1024 * 1024
        ),
        cost_estimate=pl.CostEstimate(
            flops=4 * frames * rows * across * 27 * chans * chans,
            bytes_accessed=4 * 9 * depth * chans + 4 * frames * rows * across * chans,
            transcendentals=0,
        ),
    )(latent, gain_first, flat(weight_first), bias_first, gain_second, flat(weight_second), bias_second)


def solution(mesh):
    small = mesh.shape["tile"] == 4 and mesh.shape["group"] == 8
    return jax.shard_map(
        fused_local if small else local,
        mesh=mesh,
        in_specs=(
            P(("cand", "group"), "tile", None, None),
            P(),
            P(None, None, "group", None),
            P(),
            P(),
            P(None, None, "group", None),
            P(),
        ),
        out_specs=P(("cand", "group"), "tile", None, None),
        check_vma=False,
    )
```

```python
import jax
import jax.numpy as jnp
from jax import lax
from jax.experimental import pallas as pl
from jax.experimental.pallas import tpu as pltpu
from jax.sharding import PartitionSpec as P


def shifted(value, axis, steps):
    count = lax.axis_size(axis)
    first, last = (max(0, -steps), min(count, count - steps))
    return lax.ppermute(value, axis, [(source, source + steps) for source in range(first, last)])


def with_halo(array, sides, width):
    for axis, dim in sides:
        size, length = (lax.axis_size(axis), array.shape[dim])
        up = [(i, (i + 1) % size) for i in range(size - 1)]
        down = [(j, i) for i, j in up]
        last = lax.slice_in_dim(array, length - width, length, axis=dim)
        first = lax.slice_in_dim(array, 0, width, axis=dim)
        before = lax.ppermute(last, axis, up)
        after = lax.ppermute(first, axis, down)
        array = jnp.concatenate([before, array, after], axis=dim)
    return array


def activate(values, gain):
    wide = values.astype(jnp.float32)
    scaled = wide * lax.rsqrt(jnp.mean(wide * wide, axis=-1, keepdims=True) + 1e-06) * gain
    return jax.nn.silu(scaled)


def widen(grown):
    across = grown.shape[2]
    padded = jnp.pad(grown, ((0, 0), (0, 0), (1, 1), (0, 0)))
    return jnp.concatenate([padded[:, :, k : k + across] for k in range(3)], axis=-1)


def taps(joined, piece):
    count = joined.shape[0] - 2
    tall = joined.shape[1] - 2
    across = joined.shape[2]
    inner = piece.shape[2]
    total = jnp.zeros((count * tall * across, piece.shape[3]), jnp.float32)
    for step_t in range(3):
        for step_r in range(3):
            window = joined[step_t : step_t + count, step_r : step_r + tall].reshape(-1, inner)
            total = total + jnp.dot(
                window, piece[step_t, step_r], preferred_element_type=jnp.float32
            )
    return total.reshape(count, tall, across, piece.shape[3])


def local(latent, gain_first, weight_first, bias_first, gain_second, weight_second, bias_second):
    frames, rows, width, chans = latent.shape
    depth = 1
    first = activate(latent, gain_first).astype(jnp.bfloat16)
    earlier = shifted(first[frames - 2 :], "group", 1)
    stacked = jnp.concatenate([earlier, first], axis=0)
    grown = with_halo(stacked, (("tile", 1),), depth)
    joined_first = widen(grown)
    hidden = (
        taps(joined_first, lax.all_gather(weight_first, "group", axis=2, tiled=True)) + bias_first
    )
    second = activate(hidden, gain_second)
    second = second.astype(jnp.bfloat16)
    later = shifted(second[frames - 2 :], "group", 1)
    second = jnp.concatenate([later, second], axis=0)
    second = with_halo(second, (("tile", 1),), 1)
    joined_second = widen(second)
    branch = taps(joined_second, lax.all_gather(weight_second, "group", axis=2, tiled=True))
    result = latent.astype(jnp.float32) + branch + bias_second
    return result.astype(jnp.bfloat16)


BF16, F32 = jnp.bfloat16, jnp.float32
MESH = pl.DeviceIdType.MESH
UNITS = 18
AHEAD = 3
LAG = 2


def act_slab(wide, gain):
    square = jnp.sum(wide * wide, axis=-1, keepdims=True) * (1.0 / wide.shape[-1])
    scaled = wide * lax.rsqrt(square + 1e-06) * gain
    return scaled / (1.0 + jnp.exp(-scaled))


def fused(
    latent, gain_first_in, weight_first, bias_first_in, gain_second_in, weight_second, bias_second_in, out,
    taps_all, lat, sec, cols, total, gain_first, bias_first, gain_second, bias_second,
    load_sem, lat_sem, line_sem, z_send, z_recv, xy_send, xy_recv, core_send, core_recv, halo_send, halo_recv,
):
    tile, group = lax.axis_index("tile"), lax.axis_index("group")
    tiles, groups = lax.axis_size("tile"), lax.axis_size("group")
    y, x = tile // 2, tile % 2
    z, core = group // 2, group % 2
    zs = groups // 2
    frames, rows, across, chans = latent.shape
    x_tile, y_tile = 2 * y + (1 - x), 2 * (1 - y) + x
    z_part = x + 2 * y - 3 * x * y
    x_part = x + 2 * y - 2 * x * y
    y_part = x + 2 * y - x * y
    corner = (x + y) == 2

    lat[...] = jnp.zeros_like(lat)
    sec[...] = jnp.zeros_like(sec)


    def load(at):
        source = weight_first if at < 3 else weight_second
        return pltpu.make_async_copy(
            source.at[pl.ds(3 * (2 - at % 3), 3)],
            taps_all.at[pl.ds(3 * at, 3), z, pl.ds(3 * core, 3)],
            load_sem.at[at],
        )

    line_copies = [
        pltpu.make_async_copy(source, line, line_sem.at[at])
        for at, (source, line) in enumerate(
            (
                (gain_first_in, gain_first),
                (bias_first_in, bias_first),
                (gain_second_in, gain_second),
                (bias_second_in, bias_second),
            )
        )
    ]

    lat_copy = pltpu.make_async_copy(
        latent, lat.at[pl.ds(2, frames), pl.ds(1, rows)], lat_sem
    )
    lat_copy.start()
    for at in range(UNITS // 3):
        load(at).start()
    for copy in line_copies:
        copy.start()

    barrier = pltpu.get_barrier_semaphore()
    partners = [
        ({"group": group + 2}, z < zs - 1),
        ({"group": group - 2}, z > 0),
        ({"group": group + 4}, z < zs - 2),
        ({"group": group - 4}, z > 1),
        ({"group": group + 1}, group < groups - 1),
        ({"group": group - 1}, group > 0),
        ({"tile": tile + 1}, tile < tiles - 1),
        ({"tile": tile - 1}, tile > 0),
        ({"tile": x_tile}, None),
        ({"tile": y_tile}, None),
    ]
    expected = 0
    for where, there in partners:
        if there is None:
            pl.semaphore_signal(barrier, inc=1, device_id=where, device_id_type=MESH)
            expected = expected + 1
        else:
            @pl.when(there)
            def _():
                pl.semaphore_signal(barrier, inc=1, device_id=where, device_id_type=MESH)
            expected = expected + there.astype(jnp.int32)
    pl.semaphore_wait(barrier, expected)

    def piece(unit, part, origin, where, send, recv):
        block = taps_all.at[unit, origin, 3 * core + part]
        return pltpu.make_async_remote_copy(
            src_ref=block, dst_ref=block, send_sem=send, recv_sem=recv,
            device_id=where, device_id_type=MESH,
        )

    def along_z(unit, origin, delta):
        slot = (origin - (z + delta) + zs) % zs - 1
        return piece(unit, z_part, origin, {"group": group + 2 * delta}, z_send.at[unit], z_recv.at[unit, slot])

    def along_x(unit, origin):
        return piece(unit, x_part, origin, {"tile": x_tile}, xy_send.at[unit], xy_recv.at[unit, 0])

    def along_y(unit, origin):
        return piece(unit, y_part, origin, {"tile": y_tile}, xy_send.at[unit], xy_recv.at[unit, 1])

    def wait_pieces(count, sem):
        block = taps_all.at[0, 0, pl.ds(0, count)]
        pltpu.make_async_copy(block, block, sem).wait()

    def across_cores(unit):
        block = taps_all.at[unit, :, pl.ds(3 * core, 3)]
        return pltpu.make_async_remote_copy(
            src_ref=block, dst_ref=block, send_sem=core_send.at[unit], recv_sem=core_recv.at[unit],
            device_id={"group": 2 * z + (1 - core)}, device_id_type=MESH,
        )

    at_end = (z == 0) | (z == zs - 1)
    low_side = (z < 2).astype(jnp.int32)
    inward = 2 * low_side - 1

    def own(unit):
        along_z(unit, z, inward).start()

        @pl.when(at_end)
        def _():
            along_z(unit, z, 2 * inward).start()

        @pl.when(jnp.logical_not(at_end))
        def _():
            along_z(unit, z, -inward).start()

    def hand_on(unit, origin):
        @pl.when(jnp.logical_not(corner))
        def _():
            along_x(unit, origin).start()
            along_y(unit, origin).start()

    def await_z(unit, origin):
        wait_pieces(1, z_recv.at[unit, (origin - z + zs) % zs - 1])

    def near(unit):
        @pl.when(at_end)
        def _():
            await_z(unit, z + inward)
            hand_on(unit, z + inward)

        @pl.when(jnp.logical_not(at_end))
        def _():
            await_z(unit, z + inward)
            along_z(unit, z + inward, -inward).start()
            hand_on(unit, z + inward)
            await_z(unit, z - inward)
            hand_on(unit, z - inward)
            await_z(unit, z + 2 * inward)
            along_z(unit, z + 2 * inward, -inward).start()
            hand_on(unit, z + 2 * inward)

    def far(unit):
        @pl.when(at_end)
        def _():
            for steps in (2, 3):
                await_z(unit, z + steps * inward)
                hand_on(unit, z + steps * inward)

    def halo_copies(buf, which, kind):
        late, low, high = pl.ds(frames, 2), tile > 0, tile < tiles - 1
        body = pl.ds(2, frames)
        plan = (
            ((body, rows), (body, 0), {"tile": tile + 1}, high, low),
            ((body, 1), (body, rows + 1), {"tile": tile - 1}, low, high),
            ((late,), (pl.ds(0, 2),), {"group": group + 1}, group < groups - 1, group > 0),
        )
        for at in (0, 1) if kind == "rows" else (2,):
            source, target, where, there, here = plan[at]
            copy = pltpu.make_async_remote_copy(
                src_ref=buf.at[source], dst_ref=buf.at[target],
                send_sem=halo_send.at[which, at], recv_sem=halo_recv.at[which, at],
                device_id=where, device_id_type=MESH,
            )
            yield copy, there, here

    def send_halo(buf, which, kind):
        for copy, there, _ in halo_copies(buf, which, kind):
            pl.when(there)(copy.start)

    def await_halo(buf, which, kind):
        for copy, _, here in halo_copies(buf, which, kind):
            pl.when(here)(copy.wait_recv)

    column = lax.broadcasted_iota(jnp.int32, (across, chans), 0)

    def spread(frame, row, value):
        before = jnp.where(column == 0, 0.0, pltpu.roll(value, 1, 0))
        after = jnp.where(column == across - 1, 0.0, pltpu.roll(value, across - 1, 0))
        cols[frame, row, :, 0:chans] = before.astype(BF16)
        cols[frame, row, :, chans : 2 * chans] = value.astype(BF16)
        cols[frame, row, :, 2 * chans : 3 * chans] = after.astype(BF16)

    def first_columns(frame):
        for row in range(rows + 2):
            spread(frame, row, act_slab(lat[frame, row].astype(F32), gain_first[...][None]))

    def second_values():
        def step(frame, carry):
            for row in range(rows):
                hidden = total[frame, row] + bias_first[...][None]
                sec[frame + 2, row + 1] = act_slab(hidden, gain_second[...][None]).astype(BF16)
            return carry
        lax.fori_loop(0, frames, step, 0)
        total[...] = jnp.zeros_like(total)

    def second_columns(low, high, chosen):
        def step(frame, carry):
            for row in chosen:
                spread(frame, row, sec[frame, row].astype(F32))
            return carry
        lax.fori_loop(low, high, step, 0)

    def multiply(unit):
        step_t, step_r = 2 - (unit % 9) // 3, unit % 3
        window = cols[pl.ds(step_t, frames), pl.ds(step_r, rows)].reshape(-1, 3 * chans)
        weight = taps_all[unit].reshape(3 * chans, chans)
        added = jnp.dot(window, weight, preferred_element_type=F32)
        total[...] += added.reshape(frames, rows, across, chans)

    lat_copy.wait()
    send_halo(lat, 0, "rows")
    load(0).wait()
    for unit in range(AHEAD):
        own(unit)
    total[...] = jnp.zeros_like(total)
    for at in range(1, UNITS // 3):
        load(at).wait()
    for copy in line_copies:
        copy.wait()

    def stage(index, lag, body):
        unit = index - lag

        @pl.when((unit >= 0) & (unit < UNITS))
        def _():
            body(unit)

    def direct(unit):
        @pl.when(tile != 2)
        def _():
            wait_pieces(3, xy_recv.at[unit, 0])

        @pl.when(tile != 1)
        def _():
            wait_pieces(3, xy_recv.at[unit, 1])

        @pl.when(corner)
        def _():
            for step in range(1, zs):
                along_x(unit, (z + step) % zs).start()
                along_y(unit, (z + step) % zs).start()

    def forwarded(unit):
        @pl.when(tile == 2)
        def _():
            wait_pieces(3, xy_recv.at[unit, 0])

        @pl.when(tile == 1)
        def _():
            wait_pieces(3, xy_recv.at[unit, 1])
        across_cores(unit).start()

    def compute(unit, carry):
        across_cores(unit).wait_recv()
        multiply(unit)
        return carry

    def drain(unit):
        @pl.when(at_end)
        def _():
            wait_pieces(2, z_send.at[unit])

        @pl.when(jnp.logical_not(at_end))
        def _():
            wait_pieces(4, z_send.at[unit])
        wait_pieces(2 * zs - 2, xy_send.at[unit])
        across_cores(unit).wait_send()

    half = UNITS // 2
    direct_lag = 2 * LAG
    forward_lag = direct_lag + LAG
    first_lag = forward_lag + 1
    assert frames + 2 < first_lag
    middle = half - 1 + first_lag
    drain_lag = first_lag + 4
    turns = UNITS + first_lag

    def done_by(index):
        first = jnp.clip(index - first_lag + 1, 0, half)
        second = jnp.clip(jnp.minimum(2 * (index - middle - 2), index - first_lag - half + 1), 0, half)
        return first + second

    def turn(index, carry):
        stage(index, -AHEAD, own)
        stage(index, 0, near)
        stage(index, LAG, far)
        stage(index, direct_lag, direct)
        stage(index, forward_lag, forwarded)
        stage(index, drain_lag, drain)
        lax.fori_loop(done_by(index - 1), done_by(index), compute, 0)

        @pl.when(index == 1)
        def _():
            await_halo(lat, 0, "rows")
            send_halo(lat, 0, "frames")

        @pl.when((index >= 1) & (index <= frames))
        def _():
            first_columns(index + 1)

        @pl.when(index == frames + 1)
        def _():
            await_halo(lat, 0, "frames")
            first_columns(0)

        @pl.when(index == frames + 2)
        def _():
            first_columns(1)

        @pl.when(index == middle)
        def _():
            second_values()
            send_halo(sec, 1, "rows")

        @pl.when(index == middle + 1)
        def _():
            second_columns(2, frames + 2, range(1, rows + 1))

        @pl.when(index == middle + 2)
        def _():
            await_halo(sec, 1, "rows")
            send_halo(sec, 1, "frames")
            second_columns(2, frames + 2, (0, rows + 1))

        @pl.when(index == middle + 3)
        def _():
            await_halo(sec, 1, "frames")
            second_columns(0, 2, range(rows + 2))
        return carry

    lax.fori_loop(0, turns, turn, 0)

    def finish(frame, carry):
        for row in range(rows):
            value = lat[frame + 2, row + 1].astype(F32) + total[frame, row] + bias_second[...][None]
            out[frame, row] = value.astype(BF16)
        return carry
    lax.fori_loop(0, frames, finish, 0)

    def drain_rest(unit, carry):
        drain(unit)
        return carry
    lax.fori_loop(turns - drain_lag, UNITS, drain_rest, 0)
    for which, buf in enumerate((lat, sec)):
        for kind in ("rows", "frames"):
            for copy, there, _ in halo_copies(buf, which, kind):
                pl.when(there)(copy.wait_send)


def fused_local(latent, gain_first, weight_first, bias_first, gain_second, weight_second, bias_second):
    frames, rows, across, chans = latent.shape
    depth, zs = weight_first.shape[2], lax.axis_size("group") // 2
    flat = lambda weight: weight.reshape(9, 3, depth // 3, chans)
    anywhere = pl.BlockSpec(memory_space=pl.ANY)
    return pl.pallas_call(
        fused,
        out_shape=jax.ShapeDtypeStruct(latent.shape, BF16),
        in_specs=[anywhere] * 7,
        out_specs=pl.BlockSpec(memory_space=pltpu.VMEM),
        scratch_shapes=[
            pltpu.VMEM((UNITS, zs, 6, depth // 3, chans), BF16),
            pltpu.VMEM((frames + 2, rows + 2, across, chans), BF16),
            pltpu.VMEM((frames + 2, rows + 2, across, chans), BF16),
            pltpu.VMEM((frames + 2, rows + 2, across, 3 * chans), BF16),
            pltpu.VMEM((frames, rows, across, chans), F32),
            *[pltpu.VMEM((chans,), F32)] * 4,
            pltpu.SemaphoreType.DMA((UNITS // 3,)),
            pltpu.SemaphoreType.DMA,
            pltpu.SemaphoreType.DMA((4,)),
            pltpu.SemaphoreType.DMA((UNITS,)),
            pltpu.SemaphoreType.DMA((UNITS, zs - 1)),
            pltpu.SemaphoreType.DMA((UNITS,)),
            pltpu.SemaphoreType.DMA((UNITS, 2)),
            pltpu.SemaphoreType.DMA((UNITS,)),
            pltpu.SemaphoreType.DMA((UNITS,)),
            pltpu.SemaphoreType.DMA((2, 3)),
            pltpu.SemaphoreType.DMA((2, 3)),
        ],
        compiler_params=pltpu.CompilerParams(
            collective_id=0, has_side_effects=True, vmem_limit_bytes=60 * 1024 * 1024
        ),
        cost_estimate=pl.CostEstimate(
            flops=4 * frames * rows * across * 27 * chans * chans,
            bytes_accessed=4 * 9 * depth * chans + 4 * frames * rows * across * chans,
            transcendentals=0,
        ),
    )(latent, gain_first, flat(weight_first), bias_first, gain_second, flat(weight_second), bias_second)


def solution(mesh):
    small = mesh.shape["tile"] == 4 and mesh.shape["group"] == 8
    return jax.shard_map(
        fused_local if small else local,
        mesh=mesh,
        in_specs=(
            P(("cand", "group"), "tile", None, None),
            P(),
            P(None, None, "group", None),
            P(),
            P(),
            P(None, None, "group", None),
            P(),
        ),
        out_specs=P(("cand", "group"), "tile", None, None),
        check_vma=False,
    )
```

```python
import jax
import jax.numpy as jnp
from jax import lax
from jax.experimental import pallas as pl
from jax.experimental.pallas import tpu as pltpu
from jax.sharding import PartitionSpec as P


def shifted(value, axis, steps):
    count = lax.axis_size(axis)
    first, last = (max(0, -steps), min(count, count - steps))
    return lax.ppermute(value, axis, [(source, source + steps) for source in range(first, last)])


def with_halo(array, sides, width):
    for axis, dim in sides:
        size, length = (lax.axis_size(axis), array.shape[dim])
        up = [(i, (i + 1) % size) for i in range(size - 1)]
        down = [(j, i) for i, j in up]
        last = lax.slice_in_dim(array, length - width, length, axis=dim)
        first = lax.slice_in_dim(array, 0, width, axis=dim)
        before = lax.ppermute(last, axis, up)
        after = lax.ppermute(first, axis, down)
        array = jnp.concatenate([before, array, after], axis=dim)
    return array


def activate(values, gain):
    wide = values.astype(jnp.float32)
    scaled = wide * lax.rsqrt(jnp.mean(wide * wide, axis=-1, keepdims=True) + 1e-06) * gain
    return jax.nn.silu(scaled)


def widen(grown):
    across = grown.shape[2]
    padded = jnp.pad(grown, ((0, 0), (0, 0), (1, 1), (0, 0)))
    return jnp.concatenate([padded[:, :, k : k + across] for k in range(3)], axis=-1)


def taps(joined, piece):
    count = joined.shape[0] - 2
    tall = joined.shape[1] - 2
    across = joined.shape[2]
    inner = piece.shape[2]
    total = jnp.zeros((count * tall * across, piece.shape[3]), jnp.float32)
    for step_t in range(3):
        for step_r in range(3):
            window = joined[step_t : step_t + count, step_r : step_r + tall].reshape(-1, inner)
            total = total + jnp.dot(
                window, piece[step_t, step_r], preferred_element_type=jnp.float32
            )
    return total.reshape(count, tall, across, piece.shape[3])


def local(latent, gain_first, weight_first, bias_first, gain_second, weight_second, bias_second):
    frames, rows, width, chans = latent.shape
    depth = 1
    first = activate(latent, gain_first).astype(jnp.bfloat16)
    earlier = shifted(first[frames - 2 :], "group", 1)
    stacked = jnp.concatenate([earlier, first], axis=0)
    grown = with_halo(stacked, (("tile", 1),), depth)
    joined_first = widen(grown)
    hidden = (
        taps(joined_first, lax.all_gather(weight_first, "group", axis=2, tiled=True)) + bias_first
    )
    second = activate(hidden, gain_second)
    second = second.astype(jnp.bfloat16)
    later = shifted(second[frames - 2 :], "group", 1)
    second = jnp.concatenate([later, second], axis=0)
    second = with_halo(second, (("tile", 1),), 1)
    joined_second = widen(second)
    branch = taps(joined_second, lax.all_gather(weight_second, "group", axis=2, tiled=True))
    result = latent.astype(jnp.float32) + branch + bias_second
    return result.astype(jnp.bfloat16)


BF16, F32 = jnp.bfloat16, jnp.float32
MESH = pl.DeviceIdType.MESH
UNITS = 18
AHEAD = 3
LAG = 2


def act_slab(wide, gain):
    square = jnp.sum(wide * wide, axis=-1, keepdims=True) * (1.0 / wide.shape[-1])
    scaled = wide * lax.rsqrt(square + 1e-06) * gain
    return scaled / (1.0 + jnp.exp(-scaled))


def fused(
    latent, gain_first_in, weight_first, bias_first_in, gain_second_in, weight_second, bias_second_in, out,
    taps_all, lat, sec, cols, total, gain_first, bias_first, gain_second, bias_second,
    load_sem, lat_sem, line_sem, z_send, z_recv, xy_send, xy_recv, core_send, core_recv, halo_send, halo_recv,
):
    tile, group = lax.axis_index("tile"), lax.axis_index("group")
    tiles, groups = lax.axis_size("tile"), lax.axis_size("group")
    y, x = tile // 2, tile % 2
    z, core = group // 2, group % 2
    zs = groups // 2
    frames, rows, across, chans = latent.shape
    x_tile, y_tile = 2 * y + (1 - x), 2 * (1 - y) + x
    z_part = x + 2 * y - 3 * x * y
    x_part = x + 2 * y - 2 * x * y
    y_part = x + 2 * y - x * y
    corner = (x + y) == 2

    lat[...] = jnp.zeros_like(lat)
    sec[...] = jnp.zeros_like(sec)


    def load(at):
        source = weight_first if at < 3 else weight_second
        return pltpu.make_async_copy(
            source.at[pl.ds(3 * (2 - at % 3), 3)],
            taps_all.at[pl.ds(3 * at, 3), z, pl.ds(3 * core, 3)],
            load_sem.at[at],
        )

    line_copies = [
        pltpu.make_async_copy(source, line, line_sem.at[at])
        for at, (source, line) in enumerate(
            (
                (gain_first_in, gain_first),
                (bias_first_in, bias_first),
                (gain_second_in, gain_second),
                (bias_second_in, bias_second),
            )
        )
    ]

    lat_copy = pltpu.make_async_copy(
        latent, lat.at[pl.ds(2, frames), pl.ds(1, rows)], lat_sem
    )
    lat_copy.start()
    for at in range(UNITS // 3):
        load(at).start()
    for copy in line_copies:
        copy.start()

    barrier = pltpu.get_barrier_semaphore()
    partners = [
        ({"group": group + 2}, z < zs - 1),
        ({"group": group - 2}, z > 0),
        ({"group": group + 4}, z < zs - 2),
        ({"group": group - 4}, z > 1),
        ({"group": group + 1}, group < groups - 1),
        ({"group": group - 1}, group > 0),
        ({"tile": tile + 1}, tile < tiles - 1),
        ({"tile": tile - 1}, tile > 0),
        ({"tile": x_tile}, None),
        ({"tile": y_tile}, None),
    ]
    expected = 0
    for where, there in partners:
        if there is None:
            pl.semaphore_signal(barrier, inc=1, device_id=where, device_id_type=MESH)
            expected = expected + 1
        else:
            @pl.when(there)
            def _():
                pl.semaphore_signal(barrier, inc=1, device_id=where, device_id_type=MESH)
            expected = expected + there.astype(jnp.int32)
    pl.semaphore_wait(barrier, expected)

    def piece(unit, part, origin, where, send, recv):
        block = taps_all.at[unit, origin, 3 * core + part]
        return pltpu.make_async_remote_copy(
            src_ref=block, dst_ref=block, send_sem=send, recv_sem=recv,
            device_id=where, device_id_type=MESH,
        )

    def along_z(unit, origin, delta):
        slot = (origin - (z + delta) + zs) % zs - 1
        return piece(unit, z_part, origin, {"group": group + 2 * delta}, z_send.at[unit], z_recv.at[unit, slot])

    def along_x(unit, origin):
        return piece(unit, x_part, origin, {"tile": x_tile}, xy_send.at[unit], xy_recv.at[unit, 0])

    def along_y(unit, origin):
        return piece(unit, y_part, origin, {"tile": y_tile}, xy_send.at[unit], xy_recv.at[unit, 1])

    def wait_pieces(count, sem):
        block = taps_all.at[0, 0, pl.ds(0, count)]
        pltpu.make_async_copy(block, block, sem).wait()

    def across_cores(unit):
        block = taps_all.at[unit, :, pl.ds(3 * core, 3)]
        return pltpu.make_async_remote_copy(
            src_ref=block, dst_ref=block, send_sem=core_send.at[unit], recv_sem=core_recv.at[unit],
            device_id={"group": 2 * z + (1 - core)}, device_id_type=MESH,
        )

    at_end = (z == 0) | (z == zs - 1)
    low_side = (z < 2).astype(jnp.int32)
    inward = 2 * low_side - 1

    def own(unit):
        along_z(unit, z, inward).start()

        @pl.when(at_end)
        def _():
            along_z(unit, z, 2 * inward).start()

        @pl.when(jnp.logical_not(at_end))
        def _():
            along_z(unit, z, -inward).start()

    def hand_on(unit, origin):
        @pl.when(jnp.logical_not(corner))
        def _():
            along_x(unit, origin).start()
            along_y(unit, origin).start()

    def await_z(unit, origin):
        wait_pieces(1, z_recv.at[unit, (origin - z + zs) % zs - 1])

    def near(unit):
        @pl.when(at_end)
        def _():
            await_z(unit, z + inward)
            hand_on(unit, z + inward)

        @pl.when(jnp.logical_not(at_end))
        def _():
            await_z(unit, z + inward)
            along_z(unit, z + inward, -inward).start()
            hand_on(unit, z + inward)
            await_z(unit, z - inward)
            hand_on(unit, z - inward)
            await_z(unit, z + 2 * inward)
            along_z(unit, z + 2 * inward, -inward).start()
            hand_on(unit, z + 2 * inward)

    def far(unit):
        @pl.when(at_end)
        def _():
            for steps in (2, 3):
                await_z(unit, z + steps * inward)
                hand_on(unit, z + steps * inward)

    def halo_copies(buf, which, kind):
        late, low, high = pl.ds(frames, 2), tile > 0, tile < tiles - 1
        body = pl.ds(2, frames)
        plan = (
            ((body, rows), (body, 0), {"tile": tile + 1}, high, low),
            ((body, 1), (body, rows + 1), {"tile": tile - 1}, low, high),
            ((late,), (pl.ds(0, 2),), {"group": group + 1}, group < groups - 1, group > 0),
        )
        for at in (0, 1) if kind == "rows" else (2,):
            source, target, where, there, here = plan[at]
            copy = pltpu.make_async_remote_copy(
                src_ref=buf.at[source], dst_ref=buf.at[target],
                send_sem=halo_send.at[which, at], recv_sem=halo_recv.at[which, at],
                device_id=where, device_id_type=MESH,
            )
            yield copy, there, here

    def send_halo(buf, which, kind):
        for copy, there, _ in halo_copies(buf, which, kind):
            pl.when(there)(copy.start)

    def await_halo(buf, which, kind):
        for copy, _, here in halo_copies(buf, which, kind):
            pl.when(here)(copy.wait_recv)

    column = lax.broadcasted_iota(jnp.int32, (across, chans), 0)

    def spread(frame, row, value):
        before = jnp.where(column == 0, 0.0, pltpu.roll(value, 1, 0))
        after = jnp.where(column == across - 1, 0.0, pltpu.roll(value, across - 1, 0))
        cols[frame, row, :, 0:chans] = before.astype(BF16)
        cols[frame, row, :, chans : 2 * chans] = value.astype(BF16)
        cols[frame, row, :, 2 * chans : 3 * chans] = after.astype(BF16)

    def first_columns(frame):
        for row in range(rows + 2):
            spread(frame, row, act_slab(lat[frame, row].astype(F32), gain_first[...][None]))

    def second_values():
        def step(frame, carry):
            for row in range(rows):
                hidden = total[frame, row] + bias_first[...][None]
                sec[frame + 2, row + 1] = act_slab(hidden, gain_second[...][None]).astype(BF16)
            return carry
        lax.fori_loop(0, frames, step, 0)
        total[...] = jnp.zeros_like(total)

    def second_columns(low, high, chosen):
        def step(frame, carry):
            for row in chosen:
                spread(frame, row, sec[frame, row].astype(F32))
            return carry
        lax.fori_loop(low, high, step, 0)

    def multiply(unit):
        step_t, step_r = 2 - (unit % 9) // 3, unit % 3
        window = cols[pl.ds(step_t, frames), pl.ds(step_r, rows)].reshape(-1, 3 * chans)
        weight = taps_all[unit].reshape(3 * chans, chans)
        added = jnp.dot(window, weight, preferred_element_type=F32)
        total[...] += added.reshape(frames, rows, across, chans)

    lat_copy.wait()
    send_halo(lat, 0, "rows")
    load(0).wait()
    for unit in range(AHEAD):
        own(unit)
    total[...] = jnp.zeros_like(total)
    for at in range(1, UNITS // 3):
        load(at).wait()
    for copy in line_copies:
        copy.wait()

    def stage(index, lag, body):
        unit = index - lag

        @pl.when((unit >= 0) & (unit < UNITS))
        def _():
            body(unit)

    def direct(unit):
        @pl.when(tile != 2)
        def _():
            wait_pieces(3, xy_recv.at[unit, 0])

        @pl.when(tile != 1)
        def _():
            wait_pieces(3, xy_recv.at[unit, 1])

        @pl.when(corner)
        def _():
            for step in range(1, zs):
                along_x(unit, (z + step) % zs).start()
                along_y(unit, (z + step) % zs).start()

    def forwarded(unit):
        @pl.when(tile == 2)
        def _():
            wait_pieces(3, xy_recv.at[unit, 0])

        @pl.when(tile == 1)
        def _():
            wait_pieces(3, xy_recv.at[unit, 1])
        across_cores(unit).start()

    def compute(unit, carry):
        across_cores(unit).wait_recv()
        multiply(unit)
        return carry

    def drain(unit):
        @pl.when(at_end)
        def _():
            wait_pieces(2, z_send.at[unit])

        @pl.when(jnp.logical_not(at_end))
        def _():
            wait_pieces(4, z_send.at[unit])
        wait_pieces(2 * zs - 2, xy_send.at[unit])
        across_cores(unit).wait_send()

    half = UNITS // 2
    direct_lag = 2 * LAG
    forward_lag = direct_lag + LAG
    first_lag = forward_lag + 1
    assert frames + 2 < first_lag
    middle = half - 1 + first_lag
    drain_lag = first_lag + 4
    turns = UNITS + first_lag - LAG

    def reached(index, lag):
        hurry = 2 * index - UNITS - 3 * (lag // LAG - 1)
        return jnp.clip(jnp.maximum(index - lag + 1, hurry), 0, UNITS)

    def steps(index, lag, body):
        def step(unit, carry):
            body(unit)
            return carry
        lax.fori_loop(reached(index - 1, lag), reached(index, lag), step, 0)

    def done_by(index):
        first = jnp.clip(index - first_lag + 1, 0, half)
        second = jnp.clip(jnp.minimum(2 * (index - middle - 2), reached(index - 1, forward_lag) - half), 0, half)
        return first + second

    def turn(index, carry):
        stage(index, -AHEAD, own)
        stage(index, 0, near)
        steps(index, LAG, far)
        steps(index, direct_lag, direct)
        steps(index, forward_lag, forwarded)
        stage(index, drain_lag, drain)
        lax.fori_loop(done_by(index - 1), done_by(index), compute, 0)

        @pl.when(index == 1)
        def _():
            await_halo(lat, 0, "rows")
            send_halo(lat, 0, "frames")

        @pl.when((index >= 1) & (index <= frames))
        def _():
            first_columns(index + 1)

        @pl.when(index == frames + 1)
        def _():
            await_halo(lat, 0, "frames")
            first_columns(0)

        @pl.when(index == frames + 2)
        def _():
            first_columns(1)

        @pl.when(index == middle)
        def _():
            second_values()
            send_halo(sec, 1, "rows")

        @pl.when(index == middle + 1)
        def _():
            second_columns(2, frames + 2, range(1, rows + 1))

        @pl.when(index == middle + 2)
        def _():
            await_halo(sec, 1, "rows")
            send_halo(sec, 1, "frames")
            second_columns(2, frames + 2, (0, rows + 1))

        @pl.when(index == middle + 3)
        def _():
            await_halo(sec, 1, "frames")
            second_columns(0, 2, range(rows + 2))
        return carry

    lax.fori_loop(0, turns, turn, 0)

    def finish(frame, carry):
        for row in range(rows):
            value = lat[frame + 2, row + 1].astype(F32) + total[frame, row] + bias_second[...][None]
            out[frame, row] = value.astype(BF16)
        return carry
    lax.fori_loop(0, frames, finish, 0)

    def drain_rest(unit, carry):
        drain(unit)
        return carry
    lax.fori_loop(turns - drain_lag, UNITS, drain_rest, 0)
    for which, buf in enumerate((lat, sec)):
        for kind in ("rows", "frames"):
            for copy, there, _ in halo_copies(buf, which, kind):
                pl.when(there)(copy.wait_send)


def fused_local(latent, gain_first, weight_first, bias_first, gain_second, weight_second, bias_second):
    frames, rows, across, chans = latent.shape
    depth, zs = weight_first.shape[2], lax.axis_size("group") // 2
    flat = lambda weight: weight.reshape(9, 3, depth // 3, chans)
    anywhere = pl.BlockSpec(memory_space=pl.ANY)
    return pl.pallas_call(
        fused,
        out_shape=jax.ShapeDtypeStruct(latent.shape, BF16),
        in_specs=[anywhere] * 7,
        out_specs=pl.BlockSpec(memory_space=pltpu.VMEM),
        scratch_shapes=[
            pltpu.VMEM((UNITS, zs, 6, depth // 3, chans), BF16),
            pltpu.VMEM((frames + 2, rows + 2, across, chans), BF16),
            pltpu.VMEM((frames + 2, rows + 2, across, chans), BF16),
            pltpu.VMEM((frames + 2, rows + 2, across, 3 * chans), BF16),
            pltpu.VMEM((frames, rows, across, chans), F32),
            *[pltpu.VMEM((chans,), F32)] * 4,
            pltpu.SemaphoreType.DMA((UNITS // 3,)),
            pltpu.SemaphoreType.DMA,
            pltpu.SemaphoreType.DMA((4,)),
            pltpu.SemaphoreType.DMA((UNITS,)),
            pltpu.SemaphoreType.DMA((UNITS, zs - 1)),
            pltpu.SemaphoreType.DMA((UNITS,)),
            pltpu.SemaphoreType.DMA((UNITS, 2)),
            pltpu.SemaphoreType.DMA((UNITS,)),
            pltpu.SemaphoreType.DMA((UNITS,)),
            pltpu.SemaphoreType.DMA((2, 3)),
            pltpu.SemaphoreType.DMA((2, 3)),
        ],
        compiler_params=pltpu.CompilerParams(
            collective_id=0, has_side_effects=True, vmem_limit_bytes=56 * 1024 * 1024
        ),
        cost_estimate=pl.CostEstimate(
            flops=4 * frames * rows * across * 27 * chans * chans,
            bytes_accessed=4 * 9 * depth * chans + 4 * frames * rows * across * chans,
            transcendentals=0,
        ),
    )(latent, gain_first, flat(weight_first), bias_first, gain_second, flat(weight_second), bias_second)


def solution(mesh):
    small = mesh.shape["tile"] == 4 and mesh.shape["group"] == 8
    return jax.shard_map(
        fused_local if small else local,
        mesh=mesh,
        in_specs=(
            P(("cand", "group"), "tile", None, None),
            P(),
            P(None, None, "group", None),
            P(),
            P(),
            P(None, None, "group", None),
            P(),
        ),
        out_specs=P(("cand", "group"), "tile", None, None),
        check_vma=False,
    )
```

```python
import jax
import jax.numpy as jnp
from jax import lax
from jax.experimental import pallas as pl
from jax.experimental.pallas import tpu as pltpu
from jax.sharding import PartitionSpec as P


def shifted(value, axis, steps):
    count = lax.axis_size(axis)
    first, last = (max(0, -steps), min(count, count - steps))
    return lax.ppermute(value, axis, [(source, source + steps) for source in range(first, last)])


def with_halo(array, sides, width):
    for axis, dim in sides:
        size, length = (lax.axis_size(axis), array.shape[dim])
        up = [(i, (i + 1) % size) for i in range(size - 1)]
        down = [(j, i) for i, j in up]
        last = lax.slice_in_dim(array, length - width, length, axis=dim)
        first = lax.slice_in_dim(array, 0, width, axis=dim)
        before = lax.ppermute(last, axis, up)
        after = lax.ppermute(first, axis, down)
        array = jnp.concatenate([before, array, after], axis=dim)
    return array


def activate(values, gain):
    wide = values.astype(jnp.float32)
    scaled = wide * lax.rsqrt(jnp.mean(wide * wide, axis=-1, keepdims=True) + 1e-06) * gain
    return jax.nn.silu(scaled)


def widen(grown):
    across = grown.shape[2]
    padded = jnp.pad(grown, ((0, 0), (0, 0), (1, 1), (0, 0)))
    return jnp.concatenate([padded[:, :, k : k + across] for k in range(3)], axis=-1)


def taps(joined, piece):
    count = joined.shape[0] - 2
    tall = joined.shape[1] - 2
    across = joined.shape[2]
    inner = piece.shape[2]
    total = jnp.zeros((count * tall * across, piece.shape[3]), jnp.float32)
    for step_t in range(3):
        for step_r in range(3):
            window = joined[step_t : step_t + count, step_r : step_r + tall].reshape(-1, inner)
            total = total + jnp.dot(
                window, piece[step_t, step_r], preferred_element_type=jnp.float32
            )
    return total.reshape(count, tall, across, piece.shape[3])


def local(latent, gain_first, weight_first, bias_first, gain_second, weight_second, bias_second):
    frames, rows, width, chans = latent.shape
    depth = 1
    first = activate(latent, gain_first).astype(jnp.bfloat16)
    earlier = shifted(first[frames - 2 :], "group", 1)
    stacked = jnp.concatenate([earlier, first], axis=0)
    grown = with_halo(stacked, (("tile", 1),), depth)
    joined_first = widen(grown)
    hidden = (
        taps(joined_first, lax.all_gather(weight_first, "group", axis=2, tiled=True)) + bias_first
    )
    second = activate(hidden, gain_second)
    second = second.astype(jnp.bfloat16)
    later = shifted(second[frames - 2 :], "group", 1)
    second = jnp.concatenate([later, second], axis=0)
    second = with_halo(second, (("tile", 1),), 1)
    joined_second = widen(second)
    branch = taps(joined_second, lax.all_gather(weight_second, "group", axis=2, tiled=True))
    result = latent.astype(jnp.float32) + branch + bias_second
    return result.astype(jnp.bfloat16)


BF16, F32 = jnp.bfloat16, jnp.float32
MESH = pl.DeviceIdType.MESH
UNITS = 18
AHEAD = 3
LAG = 2


def act_slab(wide, gain):
    square = jnp.sum(wide * wide, axis=-1, keepdims=True) * (1.0 / wide.shape[-1])
    scaled = wide * lax.rsqrt(square + 1e-06) * gain
    return scaled / (1.0 + jnp.exp(-scaled))


def fused(
    latent, gain_first_in, weight_first, bias_first_in, gain_second_in, weight_second, bias_second_in, out,
    taps_all, lat, sec, cols, total, gain_first, bias_first, gain_second, bias_second,
    load_sem, lat_sem, line_sem, z_send, z_recv, xy_send, xy_recv, core_send, core_recv, halo_send, halo_recv,
):
    tile, group = lax.axis_index("tile"), lax.axis_index("group")
    tiles, groups = lax.axis_size("tile"), lax.axis_size("group")
    y, x = tile // 2, tile % 2
    z, core = group // 2, group % 2
    zs = groups // 2
    frames, rows, across, chans = latent.shape
    x_tile, y_tile = 2 * y + (1 - x), 2 * (1 - y) + x
    z_part = x + 2 * y - 3 * x * y
    x_part = x + 2 * y - 2 * x * y
    y_part = x + 2 * y - x * y
    corner = (x + y) == 2

    lat[...] = jnp.zeros_like(lat)
    sec[...] = jnp.zeros_like(sec)


    def load(at):
        source = weight_first if at < 3 else weight_second
        return pltpu.make_async_copy(
            source.at[pl.ds(3 * (2 - at % 3), 3)],
            taps_all.at[pl.ds(3 * at, 3), z, pl.ds(3 * core, 3)],
            load_sem.at[at],
        )

    line_copies = [
        pltpu.make_async_copy(source, line, line_sem.at[at])
        for at, (source, line) in enumerate(
            (
                (gain_first_in, gain_first),
                (bias_first_in, bias_first),
                (gain_second_in, gain_second),
                (bias_second_in, bias_second),
            )
        )
    ]

    lat_copy = pltpu.make_async_copy(
        latent, lat.at[pl.ds(2, frames), pl.ds(1, rows)], lat_sem
    )
    lat_copy.start()
    for at in range(UNITS // 3):
        load(at).start()
    for copy in line_copies:
        copy.start()

    barrier = pltpu.get_barrier_semaphore()
    partners = [
        ({"group": group + 2}, z < zs - 1),
        ({"group": group - 2}, z > 0),
        ({"group": group + 4}, z < zs - 2),
        ({"group": group - 4}, z > 1),
        ({"group": group + 1}, group < groups - 1),
        ({"group": group - 1}, group > 0),
        ({"tile": tile + 1}, tile < tiles - 1),
        ({"tile": tile - 1}, tile > 0),
        ({"tile": x_tile}, None),
        ({"tile": y_tile}, None),
    ]
    expected = 0
    for where, there in partners:
        if there is None:
            pl.semaphore_signal(barrier, inc=1, device_id=where, device_id_type=MESH)
            expected = expected + 1
        else:
            @pl.when(there)
            def _():
                pl.semaphore_signal(barrier, inc=1, device_id=where, device_id_type=MESH)
            expected = expected + there.astype(jnp.int32)
    pl.semaphore_wait(barrier, expected)

    def piece(unit, part, origin, where, send, recv):
        block = taps_all.at[unit, origin, 3 * core + part]
        return pltpu.make_async_remote_copy(
            src_ref=block, dst_ref=block, send_sem=send, recv_sem=recv,
            device_id=where, device_id_type=MESH,
        )

    def along_z(unit, origin, delta):
        slot = (origin - (z + delta) + zs) % zs - 1
        return piece(unit, z_part, origin, {"group": group + 2 * delta}, z_send.at[unit], z_recv.at[unit, slot])

    def along_x(unit, origin):
        return piece(unit, x_part, origin, {"tile": x_tile}, xy_send.at[unit], xy_recv.at[unit, 0])

    def along_y(unit, origin):
        return piece(unit, y_part, origin, {"tile": y_tile}, xy_send.at[unit], xy_recv.at[unit, 1])

    def wait_pieces(count, sem):
        block = taps_all.at[0, 0, pl.ds(0, count)]
        pltpu.make_async_copy(block, block, sem).wait()

    def across_cores(unit):
        block = taps_all.at[unit, :, pl.ds(3 * core, 3)]
        return pltpu.make_async_remote_copy(
            src_ref=block, dst_ref=block, send_sem=core_send.at[unit], recv_sem=core_recv.at[unit],
            device_id={"group": 2 * z + (1 - core)}, device_id_type=MESH,
        )

    at_end = (z == 0) | (z == zs - 1)
    low_side = (z < 2).astype(jnp.int32)
    inward = 2 * low_side - 1

    def own(unit):
        along_z(unit, z, inward).start()

        @pl.when(at_end)
        def _():
            along_z(unit, z, 2 * inward).start()

        @pl.when(jnp.logical_not(at_end))
        def _():
            along_z(unit, z, -inward).start()

    def hand_on(unit, origin):
        @pl.when(jnp.logical_not(corner))
        def _():
            along_x(unit, origin).start()
            along_y(unit, origin).start()

    def await_z(unit, origin):
        wait_pieces(1, z_recv.at[unit, (origin - z + zs) % zs - 1])

    def near(unit):
        @pl.when(at_end)
        def _():
            await_z(unit, z + inward)
            hand_on(unit, z + inward)

        @pl.when(jnp.logical_not(at_end))
        def _():
            await_z(unit, z + inward)
            along_z(unit, z + inward, -inward).start()
            hand_on(unit, z + inward)
            await_z(unit, z - inward)
            hand_on(unit, z - inward)
            await_z(unit, z + 2 * inward)
            along_z(unit, z + 2 * inward, -inward).start()
            hand_on(unit, z + 2 * inward)

    def far(unit):
        @pl.when(at_end)
        def _():
            for steps in (2, 3):
                await_z(unit, z + steps * inward)
                hand_on(unit, z + steps * inward)

    def halo_copies(buf, which, kind):
        late, low, high = pl.ds(frames, 2), tile > 0, tile < tiles - 1
        body = pl.ds(2, frames)
        plan = (
            ((body, rows), (body, 0), {"tile": tile + 1}, high, low),
            ((body, 1), (body, rows + 1), {"tile": tile - 1}, low, high),
            ((late,), (pl.ds(0, 2),), {"group": group + 1}, group < groups - 1, group > 0),
        )
        for at in (0, 1) if kind == "rows" else (2,):
            source, target, where, there, here = plan[at]
            copy = pltpu.make_async_remote_copy(
                src_ref=buf.at[source], dst_ref=buf.at[target],
                send_sem=halo_send.at[which, at], recv_sem=halo_recv.at[which, at],
                device_id=where, device_id_type=MESH,
            )
            yield copy, there, here

    def send_halo(buf, which, kind):
        for copy, there, _ in halo_copies(buf, which, kind):
            pl.when(there)(copy.start)

    def await_halo(buf, which, kind):
        for copy, _, here in halo_copies(buf, which, kind):
            pl.when(here)(copy.wait_recv)

    column = lax.broadcasted_iota(jnp.int32, (across, chans), 0)

    def spread(frame, row, value):
        before = jnp.where(column == 0, 0.0, pltpu.roll(value, 1, 0))
        after = jnp.where(column == across - 1, 0.0, pltpu.roll(value, across - 1, 0))
        cols[frame, row, :, 0:chans] = before.astype(BF16)
        cols[frame, row, :, chans : 2 * chans] = value.astype(BF16)
        cols[frame, row, :, 2 * chans : 3 * chans] = after.astype(BF16)

    def first_columns(frame):
        for row in range(rows + 2):
            spread(frame, row, act_slab(lat[frame, row].astype(F32), gain_first[...][None]))

    def second_values():
        def step(frame, carry):
            for row in range(rows):
                hidden = total[frame, row] + bias_first[...][None]
                sec[frame + 2, row + 1] = act_slab(hidden, gain_second[...][None]).astype(BF16)
            return carry
        lax.fori_loop(0, frames, step, 0)
        total[...] = jnp.zeros_like(total)

    def second_columns(low, high, chosen):
        def step(frame, carry):
            for row in chosen:
                spread(frame, row, sec[frame, row].astype(F32))
            return carry
        lax.fori_loop(low, high, step, 0)

    def multiply(unit):
        step_t, step_r = 2 - (unit % 9) // 3, unit % 3
        window = cols[pl.ds(step_t, frames), pl.ds(step_r, rows)].reshape(-1, 3 * chans)
        weight = taps_all[unit].reshape(3 * chans, chans)
        added = jnp.dot(window, weight, preferred_element_type=F32)
        total[...] += added.reshape(frames, rows, across, chans)

    lat_copy.wait()
    send_halo(lat, 0, "rows")
    load(0).wait()
    for unit in range(AHEAD):
        own(unit)
    total[...] = jnp.zeros_like(total)
    for at in range(1, UNITS // 3):
        load(at).wait()
    for copy in line_copies:
        copy.wait()

    def stage(index, lag, body):
        unit = index - lag

        @pl.when((unit >= 0) & (unit < UNITS))
        def _():
            body(unit)

    def direct(unit):
        @pl.when(tile != 2)
        def _():
            wait_pieces(3, xy_recv.at[unit, 0])

        @pl.when(tile != 1)
        def _():
            wait_pieces(3, xy_recv.at[unit, 1])

        @pl.when(corner)
        def _():
            for step in range(1, zs):
                along_x(unit, (z + step) % zs).start()
                along_y(unit, (z + step) % zs).start()

    def forwarded(unit):
        @pl.when(tile == 2)
        def _():
            wait_pieces(3, xy_recv.at[unit, 0])

        @pl.when(tile == 1)
        def _():
            wait_pieces(3, xy_recv.at[unit, 1])
        across_cores(unit).start()

    def compute(unit, carry):
        across_cores(unit).wait_recv()
        multiply(unit)
        return carry

    def drain(unit):
        @pl.when(at_end)
        def _():
            wait_pieces(2, z_send.at[unit])

        @pl.when(jnp.logical_not(at_end))
        def _():
            wait_pieces(4, z_send.at[unit])
        wait_pieces(2 * zs - 2, xy_send.at[unit])
        across_cores(unit).wait_send()

    half = UNITS // 2
    direct_lag = 2 * LAG - 1
    forward_lag = direct_lag + LAG
    first_lag = forward_lag + 1
    assert frames < first_lag
    middle = half - 1 + first_lag
    drain_lag = first_lag + 4
    turns = UNITS + first_lag

    def done_by(index):
        first = jnp.clip(index - first_lag + 1, 0, half)
        second = jnp.clip(jnp.minimum(2 * (index - middle - 2), index - first_lag - half + 1), 0, half)
        return first + second

    def turn(index, carry):
        stage(index, -AHEAD, own)
        stage(index, 0, near)
        stage(index, LAG, far)
        stage(index, forward_lag, forwarded)
        stage(index, drain_lag, drain)
        lax.fori_loop(done_by(index - 1), done_by(index), compute, 0)
        stage(index, direct_lag, direct)

        @pl.when(index == 1)
        def _():
            await_halo(lat, 0, "rows")
            send_halo(lat, 0, "frames")

        @pl.when((index >= 1) & (index <= frames))
        def _():
            first_columns(index + 1)

        @pl.when(index == frames + 1)
        def _():
            await_halo(lat, 0, "frames")
            first_columns(0)

        @pl.when(index == frames + 2)
        def _():
            first_columns(1)

        @pl.when(index == middle)
        def _():
            second_values()
            send_halo(sec, 1, "rows")

        @pl.when(index == middle + 1)
        def _():
            second_columns(2, frames + 2, range(1, rows + 1))

        @pl.when(index == middle + 2)
        def _():
            await_halo(sec, 1, "rows")
            send_halo(sec, 1, "frames")
            second_columns(2, frames + 2, (0, rows + 1))

        @pl.when(index == middle + 3)
        def _():
            await_halo(sec, 1, "frames")
            second_columns(0, 2, range(rows + 2))
        return carry

    lax.fori_loop(0, turns, turn, 0)

    def finish(frame, carry):
        for row in range(rows):
            value = lat[frame + 2, row + 1].astype(F32) + total[frame, row] + bias_second[...][None]
            out[frame, row] = value.astype(BF16)
        return carry
    lax.fori_loop(0, frames, finish, 0)

    def drain_rest(unit, carry):
        drain(unit)
        return carry
    lax.fori_loop(turns - drain_lag, UNITS, drain_rest, 0)
    for which, buf in enumerate((lat, sec)):
        for kind in ("rows", "frames"):
            for copy, there, _ in halo_copies(buf, which, kind):
                pl.when(there)(copy.wait_send)


def fused_local(latent, gain_first, weight_first, bias_first, gain_second, weight_second, bias_second):
    frames, rows, across, chans = latent.shape
    depth, zs = weight_first.shape[2], lax.axis_size("group") // 2
    flat = lambda weight: weight.reshape(9, 3, depth // 3, chans)
    anywhere = pl.BlockSpec(memory_space=pl.ANY)
    return pl.pallas_call(
        fused,
        out_shape=jax.ShapeDtypeStruct(latent.shape, BF16),
        in_specs=[anywhere] * 7,
        out_specs=pl.BlockSpec(memory_space=pltpu.VMEM),
        scratch_shapes=[
            pltpu.VMEM((UNITS, zs, 6, depth // 3, chans), BF16),
            pltpu.VMEM((frames + 2, rows + 2, across, chans), BF16),
            pltpu.VMEM((frames + 2, rows + 2, across, chans), BF16),
            pltpu.VMEM((frames + 2, rows + 2, across, 3 * chans), BF16),
            pltpu.VMEM((frames, rows, across, chans), F32),
            *[pltpu.VMEM((chans,), F32)] * 4,
            pltpu.SemaphoreType.DMA((UNITS // 3,)),
            pltpu.SemaphoreType.DMA,
            pltpu.SemaphoreType.DMA((4,)),
            pltpu.SemaphoreType.DMA((UNITS,)),
            pltpu.SemaphoreType.DMA((UNITS, zs - 1)),
            pltpu.SemaphoreType.DMA((UNITS,)),
            pltpu.SemaphoreType.DMA((UNITS, 2)),
            pltpu.SemaphoreType.DMA((UNITS,)),
            pltpu.SemaphoreType.DMA((UNITS,)),
            pltpu.SemaphoreType.DMA((2, 3)),
            pltpu.SemaphoreType.DMA((2, 3)),
        ],
        compiler_params=pltpu.CompilerParams(
            collective_id=0, has_side_effects=True, vmem_limit_bytes=60 * 1024 * 1024
        ),
        cost_estimate=pl.CostEstimate(
            flops=4 * frames * rows * across * 27 * chans * chans,
            bytes_accessed=4 * 9 * depth * chans + 4 * frames * rows * across * chans,
            transcendentals=0,
        ),
    )(latent, gain_first, flat(weight_first), bias_first, gain_second, flat(weight_second), bias_second)


def solution(mesh):
    small = mesh.shape["tile"] == 4 and mesh.shape["group"] == 8
    return jax.shard_map(
        fused_local if small else local,
        mesh=mesh,
        in_specs=(
            P(("cand", "group"), "tile", None, None),
            P(),
            P(None, None, "group", None),
            P(),
            P(),
            P(None, None, "group", None),
            P(),
        ),
        out_specs=P(("cand", "group"), "tile", None, None),
        check_vma=False,
    )
```

```python
import jax
import jax.numpy as jnp
from jax import lax
from jax.experimental import pallas as pl
from jax.experimental.pallas import tpu as pltpu
from jax.sharding import PartitionSpec as P


def shifted(value, axis, steps):
    count = lax.axis_size(axis)
    first, last = (max(0, -steps), min(count, count - steps))
    return lax.ppermute(value, axis, [(source, source + steps) for source in range(first, last)])


def with_halo(array, sides, width):
    for axis, dim in sides:
        size, length = (lax.axis_size(axis), array.shape[dim])
        up = [(i, (i + 1) % size) for i in range(size - 1)]
        down = [(j, i) for i, j in up]
        last = lax.slice_in_dim(array, length - width, length, axis=dim)
        first = lax.slice_in_dim(array, 0, width, axis=dim)
        before = lax.ppermute(last, axis, up)
        after = lax.ppermute(first, axis, down)
        array = jnp.concatenate([before, array, after], axis=dim)
    return array


def activate(values, gain):
    wide = values.astype(jnp.float32)
    scaled = wide * lax.rsqrt(jnp.mean(wide * wide, axis=-1, keepdims=True) + 1e-06) * gain
    return jax.nn.silu(scaled)


def widen(grown):
    across = grown.shape[2]
    padded = jnp.pad(grown, ((0, 0), (0, 0), (1, 1), (0, 0)))
    return jnp.concatenate([padded[:, :, k : k + across] for k in range(3)], axis=-1)


def taps(joined, piece):
    count = joined.shape[0] - 2
    tall = joined.shape[1] - 2
    across = joined.shape[2]
    inner = piece.shape[2]
    total = jnp.zeros((count * tall * across, piece.shape[3]), jnp.float32)
    for step_t in range(3):
        for step_r in range(3):
            window = joined[step_t : step_t + count, step_r : step_r + tall].reshape(-1, inner)
            total = total + jnp.dot(
                window, piece[step_t, step_r], preferred_element_type=jnp.float32
            )
    return total.reshape(count, tall, across, piece.shape[3])


def local(latent, gain_first, weight_first, bias_first, gain_second, weight_second, bias_second):
    frames, rows, width, chans = latent.shape
    depth = 1
    first = activate(latent, gain_first).astype(jnp.bfloat16)
    earlier = shifted(first[frames - 2 :], "group", 1)
    stacked = jnp.concatenate([earlier, first], axis=0)
    grown = with_halo(stacked, (("tile", 1),), depth)
    joined_first = widen(grown)
    hidden = (
        taps(joined_first, lax.all_gather(weight_first, "group", axis=2, tiled=True)) + bias_first
    )
    second = activate(hidden, gain_second)
    second = second.astype(jnp.bfloat16)
    later = shifted(second[frames - 2 :], "group", 1)
    second = jnp.concatenate([later, second], axis=0)
    second = with_halo(second, (("tile", 1),), 1)
    joined_second = widen(second)
    branch = taps(joined_second, lax.all_gather(weight_second, "group", axis=2, tiled=True))
    result = latent.astype(jnp.float32) + branch + bias_second
    return result.astype(jnp.bfloat16)


BF16, F32 = jnp.bfloat16, jnp.float32
MESH = pl.DeviceIdType.MESH
UNITS = 18
AHEAD = 2
LAG = 2


def act_slab(wide, gain):
    square = jnp.sum(wide * wide, axis=-1, keepdims=True) * (1.0 / wide.shape[-1])
    scaled = wide * lax.rsqrt(square + 1e-06) * gain
    return scaled / (1.0 + jnp.exp(-scaled))


def fused(
    latent, gain_first_in, weight_first, bias_first_in, gain_second_in, weight_second, bias_second_in, out,
    taps_all, lat, sec, cols, total, gain_first, bias_first, gain_second, bias_second,
    load_sem, lat_sem, line_sem, z_send, z_recv, xy_send, xy_recv, core_send, core_recv, halo_send, halo_recv,
):
    tile, group = lax.axis_index("tile"), lax.axis_index("group")
    tiles, groups = lax.axis_size("tile"), lax.axis_size("group")
    y, x = tile // 2, tile % 2
    z, core = group // 2, group % 2
    zs = groups // 2
    frames, rows, across, chans = latent.shape
    x_tile, y_tile = 2 * y + (1 - x), 2 * (1 - y) + x
    z_part = x + 2 * y - 3 * x * y
    x_part = x + 2 * y - 2 * x * y
    y_part = x + 2 * y - x * y
    corner = (x + y) == 2

    lat[...] = jnp.zeros_like(lat)
    sec[...] = jnp.zeros_like(sec)


    def load(at):
        source = weight_first if at < 3 else weight_second
        return pltpu.make_async_copy(
            source.at[pl.ds(3 * (2 - at % 3), 3)],
            taps_all.at[pl.ds(3 * at, 3), z, pl.ds(3 * core, 3)],
            load_sem.at[at],
        )

    line_copies = [
        pltpu.make_async_copy(source, line, line_sem.at[at])
        for at, (source, line) in enumerate(
            (
                (gain_first_in, gain_first),
                (bias_first_in, bias_first),
                (gain_second_in, gain_second),
                (bias_second_in, bias_second),
            )
        )
    ]

    lat_copy = pltpu.make_async_copy(
        latent, lat.at[pl.ds(2, frames), pl.ds(1, rows)], lat_sem
    )
    lat_copy.start()
    for at in range(UNITS // 3):
        load(at).start()
    for copy in line_copies:
        copy.start()

    barrier = pltpu.get_barrier_semaphore()
    partners = [
        ({"group": group + 2}, z < zs - 1),
        ({"group": group - 2}, z > 0),
        ({"group": group + 4}, z < zs - 2),
        ({"group": group - 4}, z > 1),
        ({"group": group + 1}, group < groups - 1),
        ({"group": group - 1}, group > 0),
        ({"tile": tile + 1}, tile < tiles - 1),
        ({"tile": tile - 1}, tile > 0),
        ({"tile": x_tile}, None),
        ({"tile": y_tile}, None),
    ]
    expected = 0
    for where, there in partners:
        if there is None:
            pl.semaphore_signal(barrier, inc=1, device_id=where, device_id_type=MESH)
            expected = expected + 1
        else:
            @pl.when(there)
            def _():
                pl.semaphore_signal(barrier, inc=1, device_id=where, device_id_type=MESH)
            expected = expected + there.astype(jnp.int32)
    pl.semaphore_wait(barrier, expected)

    def piece(unit, part, origin, where, send, recv):
        block = taps_all.at[unit, origin, 3 * core + part]
        return pltpu.make_async_remote_copy(
            src_ref=block, dst_ref=block, send_sem=send, recv_sem=recv,
            device_id=where, device_id_type=MESH,
        )

    def along_z(unit, origin, delta):
        slot = (origin - (z + delta) + zs) % zs - 1
        return piece(unit, z_part, origin, {"group": group + 2 * delta}, z_send.at[unit], z_recv.at[unit, slot])

    def along_x(unit, origin):
        return piece(unit, x_part, origin, {"tile": x_tile}, xy_send.at[unit], xy_recv.at[unit, 0])

    def along_y(unit, origin):
        return piece(unit, y_part, origin, {"tile": y_tile}, xy_send.at[unit], xy_recv.at[unit, 1])

    def wait_pieces(count, sem):
        block = taps_all.at[0, 0, pl.ds(0, count)]
        pltpu.make_async_copy(block, block, sem).wait()

    def across_cores(unit):
        block = taps_all.at[unit, :, pl.ds(3 * core, 3)]
        return pltpu.make_async_remote_copy(
            src_ref=block, dst_ref=block, send_sem=core_send.at[unit], recv_sem=core_recv.at[unit],
            device_id={"group": 2 * z + (1 - core)}, device_id_type=MESH,
        )

    at_end = (z == 0) | (z == zs - 1)
    low_side = (z < 2).astype(jnp.int32)
    inward = 2 * low_side - 1

    def own(unit):
        along_z(unit, z, inward).start()

        @pl.when(at_end)
        def _():
            along_z(unit, z, 2 * inward).start()

        @pl.when(jnp.logical_not(at_end))
        def _():
            along_z(unit, z, -inward).start()

    def hand_on(unit, origin):
        @pl.when(jnp.logical_not(corner))
        def _():
            along_x(unit, origin).start()
            along_y(unit, origin).start()

    def await_z(unit, origin):
        wait_pieces(1, z_recv.at[unit, (origin - z + zs) % zs - 1])

    def near(unit):
        @pl.when(at_end)
        def _():
            await_z(unit, z + inward)
            hand_on(unit, z + inward)

        @pl.when(jnp.logical_not(at_end))
        def _():
            await_z(unit, z + inward)
            along_z(unit, z + inward, -inward).start()
            hand_on(unit, z + inward)
            await_z(unit, z - inward)
            hand_on(unit, z - inward)
            await_z(unit, z + 2 * inward)
            along_z(unit, z + 2 * inward, -inward).start()
            hand_on(unit, z + 2 * inward)

    def far(unit):
        @pl.when(at_end)
        def _():
            for steps in (2, 3):
                await_z(unit, z + steps * inward)
                hand_on(unit, z + steps * inward)

    def halo_copies(buf, which, kind):
        late, low, high = pl.ds(frames, 2), tile > 0, tile < tiles - 1
        body = pl.ds(2, frames)
        plan = (
            ((body, rows), (body, 0), {"tile": tile + 1}, high, low),
            ((body, 1), (body, rows + 1), {"tile": tile - 1}, low, high),
            ((late,), (pl.ds(0, 2),), {"group": group + 1}, group < groups - 1, group > 0),
        )
        for at in (0, 1) if kind == "rows" else (2,):
            source, target, where, there, here = plan[at]
            copy = pltpu.make_async_remote_copy(
                src_ref=buf.at[source], dst_ref=buf.at[target],
                send_sem=halo_send.at[which, at], recv_sem=halo_recv.at[which, at],
                device_id=where, device_id_type=MESH,
            )
            yield copy, there, here

    def send_halo(buf, which, kind):
        for copy, there, _ in halo_copies(buf, which, kind):
            pl.when(there)(copy.start)

    def await_halo(buf, which, kind):
        for copy, _, here in halo_copies(buf, which, kind):
            pl.when(here)(copy.wait_recv)

    column = lax.broadcasted_iota(jnp.int32, (across, chans), 0)

    def spread(frame, row, value):
        before = jnp.where(column == 0, 0.0, pltpu.roll(value, 1, 0))
        after = jnp.where(column == across - 1, 0.0, pltpu.roll(value, across - 1, 0))
        cols[frame, row, :, 0:chans] = before.astype(BF16)
        cols[frame, row, :, chans : 2 * chans] = value.astype(BF16)
        cols[frame, row, :, 2 * chans : 3 * chans] = after.astype(BF16)

    def first_columns(frame):
        for row in range(rows + 2):
            spread(frame, row, act_slab(lat[frame, row].astype(F32), gain_first[...][None]))

    def second_values():
        def step(frame, carry):
            for row in range(rows):
                hidden = total[frame, row] + bias_first[...][None]
                sec[frame + 2, row + 1] = act_slab(hidden, gain_second[...][None]).astype(BF16)
            return carry
        lax.fori_loop(0, frames, step, 0)
        total[...] = jnp.zeros_like(total)

    def second_columns(low, high, chosen):
        def step(frame, carry):
            for row in chosen:
                spread(frame, row, sec[frame, row].astype(F32))
            return carry
        lax.fori_loop(low, high, step, 0)

    def multiply(unit):
        step_t, step_r = 2 - (unit % 9) // 3, unit % 3
        window = cols[pl.ds(step_t, frames), pl.ds(step_r, rows)].reshape(-1, 3 * chans)
        weight = taps_all[unit].reshape(3 * chans, chans)
        added = jnp.dot(window, weight, preferred_element_type=F32)
        total[...] += added.reshape(frames, rows, across, chans)

    lat_copy.wait()
    send_halo(lat, 0, "rows")
    load(0).wait()
    for unit in range(AHEAD):
        own(unit)
    total[...] = jnp.zeros_like(total)
    for at in range(1, UNITS // 3):
        load(at).wait()
    for copy in line_copies:
        copy.wait()

    def stage(index, lag, body):
        unit = index - lag

        @pl.when((unit >= 0) & (unit < UNITS))
        def _():
            body(unit)

    def direct(unit):
        @pl.when(tile != 2)
        def _():
            wait_pieces(3, xy_recv.at[unit, 0])

        @pl.when(tile != 1)
        def _():
            wait_pieces(3, xy_recv.at[unit, 1])

        @pl.when(corner)
        def _():
            for step in range(1, zs):
                along_x(unit, (z + step) % zs).start()
                along_y(unit, (z + step) % zs).start()

    def forwarded(unit):
        @pl.when(tile == 2)
        def _():
            wait_pieces(3, xy_recv.at[unit, 0])

        @pl.when(tile == 1)
        def _():
            wait_pieces(3, xy_recv.at[unit, 1])
        across_cores(unit).start()

    def compute(unit, carry):
        across_cores(unit).wait_recv()
        multiply(unit)
        return carry

    def drain(unit):
        @pl.when(at_end)
        def _():
            wait_pieces(2, z_send.at[unit])

        @pl.when(jnp.logical_not(at_end))
        def _():
            wait_pieces(4, z_send.at[unit])
        wait_pieces(2 * zs - 2, xy_send.at[unit])
        across_cores(unit).wait_send()

    half = UNITS // 2
    direct_lag = 2 * LAG
    forward_lag = direct_lag + LAG
    first_lag = forward_lag + 1
    assert frames + 2 < first_lag
    middle = half - 1 + first_lag
    drain_lag = first_lag + 4
    turns = UNITS + first_lag

    def done_by(index):
        first = jnp.clip(index - first_lag + 1, 0, half)
        second = jnp.clip(jnp.minimum(2 * (index - middle - 2), index - first_lag - half + 1), 0, half)
        return first + second

    def turn(index, carry):
        stage(index, -AHEAD, own)
        stage(index, 0, near)
        stage(index, LAG, far)
        stage(index, direct_lag, direct)
        stage(index, forward_lag, forwarded)
        stage(index, drain_lag, drain)
        lax.fori_loop(done_by(index - 1), done_by(index), compute, 0)

        @pl.when(index == 1)
        def _():
            await_halo(lat, 0, "rows")
            send_halo(lat, 0, "frames")

        @pl.when((index >= 1) & (index <= frames))
        def _():
            first_columns(index + 1)

        @pl.when(index == frames + 1)
        def _():
            await_halo(lat, 0, "frames")
            first_columns(0)

        @pl.when(index == frames + 2)
        def _():
            first_columns(1)

        @pl.when(index == middle)
        def _():
            second_values()
            send_halo(sec, 1, "rows")

        @pl.when(index == middle + 1)
        def _():
            second_columns(2, frames + 2, range(1, rows + 1))

        @pl.when(index == middle + 2)
        def _():
            await_halo(sec, 1, "rows")
            send_halo(sec, 1, "frames")
            second_columns(2, frames + 2, (0, rows + 1))

        @pl.when(index == middle + 3)
        def _():
            await_halo(sec, 1, "frames")
            second_columns(0, 2, range(rows + 2))
        return carry

    lax.fori_loop(0, turns, turn, 0)

    def finish(frame, carry):
        for row in range(rows):
            value = lat[frame + 2, row + 1].astype(F32) + total[frame, row] + bias_second[...][None]
            out[frame, row] = value.astype(BF16)
        return carry
    lax.fori_loop(0, frames, finish, 0)

    def drain_rest(unit, carry):
        drain(unit)
        return carry
    lax.fori_loop(turns - drain_lag, UNITS, drain_rest, 0)
    for which, buf in enumerate((lat, sec)):
        for kind in ("rows", "frames"):
            for copy, there, _ in halo_copies(buf, which, kind):
                pl.when(there)(copy.wait_send)


def fused_local(latent, gain_first, weight_first, bias_first, gain_second, weight_second, bias_second):
    frames, rows, across, chans = latent.shape
    depth, zs = weight_first.shape[2], lax.axis_size("group") // 2
    flat = lambda weight: weight.reshape(9, 3, depth // 3, chans)
    anywhere = pl.BlockSpec(memory_space=pl.ANY)
    return pl.pallas_call(
        fused,
        out_shape=jax.ShapeDtypeStruct(latent.shape, BF16),
        in_specs=[anywhere] * 7,
        out_specs=pl.BlockSpec(memory_space=pltpu.VMEM),
        scratch_shapes=[
            pltpu.VMEM((UNITS, zs, 6, depth // 3, chans), BF16),
            pltpu.VMEM((frames + 2, rows + 2, across, chans), BF16),
            pltpu.VMEM((frames + 2, rows + 2, across, chans), BF16),
            pltpu.VMEM((frames + 2, rows + 2, across, 3 * chans), BF16),
            pltpu.VMEM((frames, rows, across, chans), F32),
            *[pltpu.VMEM((chans,), F32)] * 4,
            pltpu.SemaphoreType.DMA((UNITS // 3,)),
            pltpu.SemaphoreType.DMA,
            pltpu.SemaphoreType.DMA((4,)),
            pltpu.SemaphoreType.DMA((UNITS,)),
            pltpu.SemaphoreType.DMA((UNITS, zs - 1)),
            pltpu.SemaphoreType.DMA((UNITS,)),
            pltpu.SemaphoreType.DMA((UNITS, 2)),
            pltpu.SemaphoreType.DMA((UNITS,)),
            pltpu.SemaphoreType.DMA((UNITS,)),
            pltpu.SemaphoreType.DMA((2, 3)),
            pltpu.SemaphoreType.DMA((2, 3)),
        ],
        compiler_params=pltpu.CompilerParams(
            collective_id=0, has_side_effects=True, vmem_limit_bytes=60 * 1024 * 1024
        ),
        cost_estimate=pl.CostEstimate(
            flops=4 * frames * rows * across * 27 * chans * chans,
            bytes_accessed=4 * 9 * depth * chans + 4 * frames * rows * across * chans,
            transcendentals=0,
        ),
    )(latent, gain_first, flat(weight_first), bias_first, gain_second, flat(weight_second), bias_second)


def solution(mesh):
    small = mesh.shape["tile"] == 4 and mesh.shape["group"] == 8
    return jax.shard_map(
        fused_local if small else local,
        mesh=mesh,
        in_specs=(
            P(("cand", "group"), "tile", None, None),
            P(),
            P(None, None, "group", None),
            P(),
            P(),
            P(None, None, "group", None),
            P(),
        ),
        out_specs=P(("cand", "group"), "tile", None, None),
        check_vma=False,
    )
```
